32 devices in a mesh: pole: 1, prow: 8 (over y, x, core), pcol: 4 (over z).
Axes of the slice: x: 2, y: 2, z: 4, core: 2. Of those that a mesh axis runs over, the one named last changes fastest.
Arguments:
- hamiltonian: bfloat16 [6144, 6144], P(('prow', 'pcol')), may hold values from -2 to 32, as said below
- margin: bfloat16 [6144, 6144], P(('prow', 'pcol')), may hold values from -1 to 1, as said below
- pole_shift: float32 [2], P('pole'), may hold values from 0.3 to 1.5
- row_map: int32 [6144], P('prow'), may hold values from 0 to 6143, as said below
- parent: int32 [48], replicated, may hold values from 1 to 48, as said below
Outputs:
- factored: float32 [2, 6144, 6144], P('pole', 'prow', 'pcol')
The draws below stay inside these ranges and needn't reach their ends.
Inputs may be any that keep to these rules, and one draw needn't show every extreme that they name: For each aligned block of 768 rows, row_map maps the block's rows one to one onto the same block's indices. parent[s] is greater than s; the value 48 marks a root. Supernode 0's parent is 1 and the last supernode is a root. `hamiltonian`: as a matrix over orbitals it is symmetric. `margin`: as a matrix over orbitals it is symmetric, with ones on its diagonal.
All inputs are finite; a program needn't handle non-finite values.
Results may differ from the reference program's by a relative error of at most 0.0023.
Values may be sent and summed in bfloat16 or wider, within the bound.
A program may use at most 128 MiB of HBM per device.

```python
import jax
import jax.numpy as jnp
from jax import lax

SN = 128
RB = 6
STEPS = 3
NSI = 4
NBW = 48
CB = 12
NO = 6144
N_PROW = 8
N_PCOL = 4


def orbital_order(key):
    base_key = jax.random.fold_in(key, 101)
    span_rows = RB * SN
    groups_count = NO // span_rows
    group_keys = jax.random.split(base_key, groups_count)
    shuffles = jax.vmap(lambda group_key: jax.random.permutation(group_key, span_rows))(group_keys)
    offsets = jnp.arange(groups_count, dtype=jnp.int32) * span_rows
    return (shuffles.astype(jnp.int32) + offsets[:, None]).reshape(NO)


def natural_symmetric(key, intra, inter, diag_lo, diag_hi):
    first_key, second_key = jax.random.split(key)
    noise = jax.random.uniform(first_key, (NO, NO), jnp.float32, -1.0, 1.0)
    mirrored = 0.5 * (noise + noise.T)
    nodes = jnp.arange(NO, dtype=jnp.int32) // SN
    scaled = mirrored * jnp.where(nodes[:, None] == nodes[None, :], intra, inter)
    onsite = jax.random.uniform(second_key, (NO,), jnp.float32, diag_lo, diag_hi)
    positions = jnp.arange(NO, dtype=jnp.int32)
    return jnp.where(positions[:, None] == positions[None, :], onsite[None, :], scaled)


def orbital_layout(key, natural_matrix):
    row_order = orbital_order(key)
    stored_place = jnp.arange(NO, dtype=jnp.int32)
    span_rows = RB * SN
    span_cols = CB * SN
    grid_rows = NBW // RB
    grid_cols = NBW // CB
    row_natural = (stored_place % span_rows // SN * grid_rows + stored_place // span_rows) * SN + stored_place % SN
    col_natural = (stored_place % span_cols // SN * grid_cols + stored_place // span_cols) * SN + stored_place % SN
    orbital_natural = jnp.zeros((NO,), jnp.int32).at[row_order].set(row_natural)
    return natural_matrix[orbital_natural][:, col_natural]


def draw_hamiltonian(key, part):
    return orbital_layout(key, natural_symmetric(jax.random.fold_in(key, 202), 1.3, 0.65, 16.0, 32.0)).astype(jnp.bfloat16)


def draw_margin(key, part):
    return orbital_layout(key, natural_symmetric(jax.random.fold_in(key, 303), 0.25, 0.08, 1.0, 1.0)).astype(jnp.bfloat16)


def draw_row_map(key, part):
    return orbital_order(key)


def draw_parent(key, part):
    node_index = jnp.arange(NBW, dtype=jnp.int32)
    reach_limit = jnp.where(node_index == 0, 1, jnp.minimum(NBW - node_index, 5))
    random_bits = jax.random.randint(jax.random.fold_in(key, 404), (NBW,), 0, 1 << 20, dtype=jnp.int32)
    return (node_index + random_bits % reach_limit + 1).astype(jnp.int32)


def setup_inputs(seed: int = 0, part: int = 0) -> dict:
    splits = jax.random.split(jax.random.key(seed), 6)
    part_keys = jax.random.split(jax.random.fold_in(splits[5], part), 6)
    return {
        "hamiltonian": draw_hamiltonian(jax.random.fold_in(splits[5], 71), part),
        "margin": draw_margin(jax.random.fold_in(splits[5], 71), part),
        "pole_shift": jnp.clip(jax.random.uniform(part_keys[2], (2,), jnp.float32, 0.3, 1.5), 0.3, 1.5),
        "row_map": draw_row_map(jax.random.fold_in(splits[5], 71), part),
        "parent": draw_parent(jax.random.fold_in(splits[5], 71), part),
    }


def complex_product(left_pair, right_pair):
    highest = lax.Precision.HIGHEST
    real_part = jnp.dot(left_pair[0], right_pair[0], precision=highest, preferred_element_type=jnp.float32) - jnp.dot(left_pair[1], right_pair[1], precision=highest, preferred_element_type=jnp.float32)
    imag_part = jnp.dot(left_pair[0], right_pair[1], precision=highest, preferred_element_type=jnp.float32) + jnp.dot(left_pair[1], right_pair[0], precision=highest, preferred_element_type=jnp.float32)
    return jnp.stack([real_part, imag_part])


def structure(parent, node_count):
    node_index = jnp.arange(node_count, dtype=jnp.int32)
    reached = (parent[:, None] == node_index[None, :]).astype(jnp.int32)
    for level_index in range(node_count.bit_length()):
        reached = jnp.minimum(reached + jnp.dot(reached, reached), 1)
    diagonal_ones = (node_index[:, None] == node_index[None, :]).astype(jnp.int32)
    return jnp.minimum(diagonal_ones + reached + reached.T, 1)


def invert_pivot(pivot, sweeps):
    pivot_size = pivot.shape[-1]
    places = jnp.arange(pivot_size, dtype=jnp.int32)
    identity_real = (places[:, None] == places[None, :]).astype(jnp.float32)
    diag_real = jnp.diagonal(pivot[0])
    diag_imag = jnp.diagonal(pivot[1])
    modulus = diag_real * diag_real + diag_imag * diag_imag
    approx = jnp.stack([identity_real * (diag_real / modulus)[None, :], identity_real * (-diag_imag / modulus)[None, :]])
    for sweep_index in range(sweeps):
        product = complex_product(pivot, approx)
        residue = jnp.stack([2.0 * identity_real - product[0], -product[1]])
        approx = complex_product(approx, residue)
    return approx


def reference(hamiltonian, margin, pole_shift, row_map, parent):
    natural = jnp.arange(NO, dtype=jnp.int32)
    supernode = natural // SN
    within = natural % SN
    row_place = ((supernode % N_PROW) * RB + supernode // N_PROW) * SN + within
    col_place = ((supernode % N_PCOL) * CB + supernode // N_PCOL) * SN + within
    ham_rows = hamiltonian[row_map].astype(jnp.float32)
    over_rows = margin[row_map].astype(jnp.float32)
    real_part = (ham_rows - pole_shift[0] * over_rows)[row_place][:, col_place]
    imag_part = (-pole_shift[1] * over_rows)[row_place][:, col_place]
    pattern = structure(parent, NBW)
    pattern_full = jnp.repeat(jnp.repeat(pattern, SN, axis=0), SN, axis=1).astype(jnp.float32)
    matrix = jnp.stack([real_part, imag_part]) * pattern_full[None]
    for elimination in range(STEPS):
        lower_edge = elimination * SN
        upper_edge = lower_edge + SN
        inverse = invert_pivot(matrix[:, lower_edge:upper_edge, lower_edge:upper_edge], NSI)
        factor = complex_product(matrix[:, upper_edge:, lower_edge:upper_edge], inverse)
        update = complex_product(factor, matrix[:, lower_edge:upper_edge, upper_edge:])
        matrix = matrix.at[:, upper_edge:, upper_edge:].add(-update)
        matrix = matrix.at[:, upper_edge:, lower_edge:upper_edge].set(factor)
    stored_place = jnp.arange(NO, dtype=jnp.int32)
    span_rows = RB * SN
    span_cols = CB * SN
    row_natural = (((stored_place % span_rows) // SN) * N_PROW + stored_place // span_rows) * SN + stored_place % SN
    col_natural = (((stored_place % span_cols) // SN) * N_PCOL + stored_place // span_cols) * SN + stored_place % SN
    return matrix[:, row_natural][:, :, col_natural]
```

```python
import functools

import jax
import jax.numpy as jnp
from jax import lax
from jax.experimental import pallas as pl
from jax.experimental.pallas import tpu as pltpu
from jax.sharding import PartitionSpec as P

SN = 128
STEPS = 3
NSI = 4
PAN = STEPS * SN
VMEM_LIMIT = 50 * 1024 * 1024
MESH = pl.DeviceIdType.MESH


def structure(parent, node_count):
    node_index = jnp.arange(node_count, dtype=jnp.int32)
    reached = (parent[:, None] == node_index[None, :]).astype(jnp.bfloat16)
    for level_index in range(node_count.bit_length()):
        hop = jnp.dot(reached, reached, preferred_element_type=jnp.float32)
        reached = jnp.minimum(reached.astype(jnp.float32) + hop, 1.0).astype(jnp.bfloat16)
    reached = reached.astype(jnp.float32)
    same = (node_index[:, None] == node_index[None, :]).astype(jnp.float32)
    return jnp.minimum(same + reached + reached.T, 1.0)


def line_gather_kernel(n, mine_ref, out_ref, local_sem, up_sem, down_sem, recv_sem):
    me = lax.axis_index("pcol")
    row = lax.axis_index("prow")
    pole = lax.axis_index("pole")
    barrier = pltpu.get_barrier_semaphore()

    @pl.when(me + 1 < n)
    def _():
        pl.semaphore_signal(barrier, inc=1, device_id=(pole, row, me + 1), device_id_type=MESH)

    @pl.when(me >= 1)
    def _():
        pl.semaphore_signal(barrier, inc=1, device_id=(pole, row, me - 1), device_id_type=MESH)

    pl.semaphore_wait(barrier, jnp.where(me + 1 < n, 1, 0) + jnp.where(me >= 1, 1, 0))

    local = pltpu.make_async_copy(mine_ref, out_ref.at[me], local_sem)
    local.start()
    local.wait()

    def send(slot, target, sems):
        return pltpu.make_async_remote_copy(
            src_ref=out_ref.at[slot],
            dst_ref=out_ref.at[slot],
            send_sem=sems.at[slot],
            recv_sem=recv_sem.at[slot],
            device_id=(pole, row, target),
            device_id_type=MESH,
        )

    for step in range(n):
        low = me - step
        high = me + step
        if step:

            @pl.when(low >= 0)
            def _():
                send(low, me, up_sem).wait_recv()

        @pl.when((low >= 0) & (me + 1 < n))
        def _():
            send(low, me + 1, up_sem).start()

        if step:

            @pl.when(high < n)
            def _():
                send(high, me, down_sem).wait_recv()

        @pl.when((high < n) & (me >= 1))
        def _():
            send(high, me - 1, down_sem).start()

    for step in range(n):
        low = me - step
        high = me + step

        @pl.when((low >= 0) & (me + 1 < n))
        def _():
            send(low, me + 1, up_sem).wait_send()

        @pl.when((high < n) & (me >= 1))
        def _():
            send(high, me - 1, down_sem).wait_send()


def line_gather(mine, n):
    return pl.pallas_call(
        functools.partial(line_gather_kernel, n),
        out_shape=jax.ShapeDtypeStruct((n,) + mine.shape, mine.dtype),
        in_specs=[pl.BlockSpec(memory_space=pl.ANY)],
        out_specs=pl.BlockSpec(memory_space=pl.ANY),
        scratch_shapes=[
            pltpu.SemaphoreType.DMA,
            pltpu.SemaphoreType.DMA((n,)),
            pltpu.SemaphoreType.DMA((n,)),
            pltpu.SemaphoreType.DMA((n,)),
        ],
        compiler_params=pltpu.CompilerParams(collective_id=0, has_side_effects=True),
        cost_estimate=pl.CostEstimate(flops=0, bytes_accessed=40_000_000, transcendentals=0),
    )(mine)


def tree_kernel(n, groups, pcols, panel_ref, *rest):
    items = groups + STEPS
    outs = rest[:items]
    local_sem, send_sem, recv_sem = rest[items:]
    me = lax.axis_index("prow")
    col = lax.axis_index("pcol")
    pole = lax.axis_index("pole")
    bits = n.bit_length() - 1
    bit = lambda value, b: (value // (1 << b)) % 2
    partner = lambda b: me + (1 << b) * (1 - 2 * bit(me, b))
    barrier = pltpu.get_barrier_semaphore()
    for b in range(bits):
        pl.semaphore_signal(barrier, inc=1, device_id=(pole, partner(b), col), device_id_type=MESH)
    pl.semaphore_wait(barrier, bits)
    roots = [(col + j * pcols) % n for j in range(groups)] + list(range(STEPS))
    forward = list(range(1, bits)) + [0]
    backward = list(range(bits - 1, 0, -1)) + [0]
    orders = [backward if i % 2 else forward for i in range(items)]
    for i in range(items):

        @pl.when(me == roots[i])
        def _():
            source = panel_ref if i < groups else panel_ref.at[:, 0:SN]
            copy = pltpu.make_async_copy(source, outs[i], local_sem.at[i])
            copy.start()
            copy.wait()

    def send(i, stage):
        return pltpu.make_async_remote_copy(
            src_ref=outs[i],
            dst_ref=outs[i],
            send_sem=send_sem.at[i, stage],
            recv_sem=recv_sem.at[i],
            device_id=(pole, partner(orders[i][stage]), col),
            device_id_type=MESH,
        )

    def relative(i, stage):
        return (bit(me, orders[i][stage]) + bit(roots[i], orders[i][stage])) % 2

    def later(i, stage):
        total = 0
        for k in range(stage, bits):
            total = total + relative(i, k)
        return total

    sequence = list(range(groups, items)) + list(range(groups))
    for stage in range(bits):
        for i in sequence:

            @pl.when(later(i, stage) == 0)
            def _():
                send(i, stage).start()

        for i in sequence:

            @pl.when((relative(i, stage) == 1) & (later(i, stage) == 1))
            def _():
                send(i, stage).wait_recv()

    for stage in range(bits):
        for i in sequence:

            @pl.when(later(i, stage) == 0)
            def _():
                send(i, stage).wait_send()


def tree(panel, n, groups, pcols):
    bits = n.bit_length() - 1
    items = groups + STEPS
    shapes = [jax.ShapeDtypeStruct(panel.shape, panel.dtype)] * groups + [
        jax.ShapeDtypeStruct((2, SN, PAN), panel.dtype)
    ] * STEPS
    return pl.pallas_call(
        functools.partial(tree_kernel, n, groups, pcols),
        out_shape=shapes,
        in_specs=[pl.BlockSpec(memory_space=pl.ANY)],
        out_specs=[pl.BlockSpec(memory_space=pl.ANY)] * items,
        scratch_shapes=[
            pltpu.SemaphoreType.DMA((items,)),
            pltpu.SemaphoreType.DMA((items, bits)),
            pltpu.SemaphoreType.DMA((items,)),
        ],
        compiler_params=pltpu.CompilerParams(collective_id=1, has_side_effects=True),
        cost_estimate=pl.CostEstimate(flops=0, bytes_accessed=60_000_000, transcendentals=0),
    )(panel)


def real_form(pair):
    left, right = pair[:, :SN], pair[:, SN:]
    return jnp.concatenate([pair, jnp.concatenate([-right, left], axis=1)], axis=0)


def panel_kernel(chunk, high, wide, pivot_ref, node_ref, rows_ref, factor_ref, real_ref, imag_ref, inv, step_b, piv):
    exact = functools.partial(
        jnp.dot, precision=lax.Precision.HIGHEST, preferred_element_type=jnp.float32
    )
    piv[...] = pivot_ref[...]
    place_r = lax.broadcasted_iota(jnp.int32, (SN, SN), 0)
    place_c = lax.broadcasted_iota(jnp.int32, (SN, SN), 1)
    eye = (place_r == place_c).astype(jnp.float32)
    zero = jnp.zeros_like(eye)
    two = 2.0 * real_form(jnp.concatenate([eye, zero], axis=1))
    pairs = [(0, 1), (0, 2), (1, 2)]
    for t in range(STEPS):
        here = slice(t * SN, (t + 1) * SN)
        cols = slice(2 * t * SN, 2 * (t + 1) * SN)
        pivot = piv[here, cols]
        full = real_form(pivot)
        diag_r = jnp.sum(eye * pivot[:, :SN], axis=0, keepdims=True)
        diag_i = jnp.sum(eye * pivot[:, SN:], axis=0, keepdims=True)
        modulus = diag_r * diag_r + diag_i * diag_i
        approx = real_form(
            jnp.concatenate([eye * (diag_r / modulus), eye * (-diag_i / modulus)], axis=1)
        )
        for sweep in range(NSI):
            approx = exact(approx, two - exact(full, approx))
        inv[t] = approx.astype(jnp.bfloat16)
        if t + 1 < STEPS:
            below = slice((t + 1) * SN, STEPS * SN)
            factor = exact(piv[below, cols], approx)
            for t2 in range(t + 1, STEPS):
                cols2 = slice(2 * t2 * SN, 2 * (t2 + 1) * SN)
                link = real_form(piv[here, cols2])
                step_b[pairs.index((t, t2))] = link.astype(jnp.bfloat16)
                piv[below, cols2] = piv[below, cols2] - exact(factor, link)

    def work(start):
        span = pl.ds(start, chunk)
        node = node_ref[span, :]
        blocks = [rows_ref[span, 2 * t * SN : 2 * (t + 1) * SN] for t in range(STEPS)]
        factors = []
        kept = []
        for t in range(STEPS):
            below = node > t
            now = blocks[t].astype(jnp.bfloat16)
            factor = jnp.dot(now, inv[t], preferred_element_type=jnp.float32)
            factor = jnp.where(below, factor, 0.0).astype(jnp.bfloat16)
            for t2 in range(t + 1, STEPS):
                blocks[t2] = blocks[t2] - jnp.dot(
                    factor, step_b[pairs.index((t, t2))], preferred_element_type=jnp.float32
                )
            factors.append(factor)
            kept.append(jnp.where(below, blocks[t], 0.0))
        return factors, kept

    @pl.loop(0, high // chunk)
    def _(k):
        start = pl.multiple_of(k * chunk, chunk)
        factors, kept = work(start)
        for t in range(STEPS):
            factor_ref[pl.ds(start, chunk), 2 * t * SN : 2 * (t + 1) * SN] = factors[t]

    @pl.loop(0, wide // chunk)
    def _(k):
        start = pl.multiple_of(k * chunk, chunk)
        factors, kept = work(pl.multiple_of(high + start, chunk))
        for t in range(STEPS):
            re, im = kept[t][:, :SN], kept[t][:, SN:]
            span = pl.ds(start, chunk)
            cols = slice(2 * t * SN, 2 * (t + 1) * SN)
            real_ref[span, cols] = jnp.concatenate([re, -im], axis=1).astype(jnp.bfloat16)
            imag_ref[span, cols] = jnp.concatenate([im, re], axis=1).astype(jnp.bfloat16)


def panels(pivot, nodes, rows, high, wide):
    chunk = 256
    bf = jnp.bfloat16
    return pl.pallas_call(
        functools.partial(panel_kernel, chunk, high, wide),
        out_shape=[
            jax.ShapeDtypeStruct((high, 2 * PAN), bf),
            jax.ShapeDtypeStruct((wide, 2 * PAN), bf),
            jax.ShapeDtypeStruct((wide, 2 * PAN), bf),
        ],
        in_specs=[pl.BlockSpec(memory_space=pltpu.VMEM)] * 3,
        out_specs=[pl.BlockSpec(memory_space=pltpu.VMEM)] * 3,
        scratch_shapes=[
            pltpu.VMEM((STEPS, 2 * SN, 2 * SN), bf),
            pltpu.VMEM((3, 2 * SN, 2 * SN), bf),
            pltpu.VMEM((PAN, 2 * PAN), jnp.float32),
        ],
        compiler_params=pltpu.CompilerParams(vmem_limit_bytes=VMEM_LIMIT),
        cost_estimate=pl.CostEstimate(
            flops=20_000_000_000, bytes_accessed=20_000_000, transcendentals=0
        ),
    )(pivot, nodes, rows)


def update_kernel(tile, shift_ref, keep_ref, block_ref, map_ref, node_ref, factor_ref, real_ref, imag_ref, own_ref, mine_ref, out_ref, pick):
    j = pl.program_id(0)
    high = map_ref.shape[0]
    blocks, _, share, _ = block_ref.shape

    @pl.when(j == 0)
    def _():
        place = lax.broadcasted_iota(jnp.int32, (high, high), 1)
        pick[...] = (place == map_ref[...]).astype(jnp.bfloat16)

    nt = (((1,), (1,)), ((), ()))
    factor = factor_ref[...]
    ham = jnp.dot(
        pick[...], block_ref[:, 0].reshape(high, tile), preferred_element_type=jnp.float32
    )
    over = jnp.dot(
        pick[...], block_ref[:, 1].reshape(high, tile), preferred_element_type=jnp.float32
    )
    up_r = lax.dot_general(factor, real_ref[...], nt, preferred_element_type=jnp.float32)
    up_i = lax.dot_general(factor, imag_ref[...], nt, preferred_element_type=jnp.float32)
    zr, zi = shift_ref[0], shift_ref[1]
    for a in range(high // SN):
        for b in range(tile // SN):
            ra, cb = slice(a * SN, (a + 1) * SN), slice(b * SN, (b + 1) * SN)
            keep = keep_ref[a, j * (tile // SN) + b] > 0.5
            h, s = ham[ra, cb], over[ra, cb]
            out_ref[0, ra, cb] = jnp.where(keep, h - zr * s, 0.0) - up_r[ra, cb]
            out_ref[1, ra, cb] = jnp.where(keep, -zi * s, 0.0) - up_i[ra, cb]

    @pl.when(j == 0)
    def _():
        take = node_ref[...] > mine_ref[0]
        for p in range(2):
            own = own_ref[:, p * SN : (p + 1) * SN].astype(jnp.float32)
            out_ref[p, :, 0:SN] = jnp.where(take, own, out_ref[p, :, 0:SN])


def update(shift, keep, block, row_places, row_owner, factor, real, imag, own, mine):
    blocks, _, share, wide = block.shape
    high = blocks * share
    tile = 256
    smem = pl.BlockSpec(memory_space=pltpu.SMEM)
    whole = lambda shape: pl.BlockSpec(shape, lambda j: (0,) * len(shape))
    return pl.pallas_call(
        functools.partial(update_kernel, tile),
        grid=(wide // tile,),
        out_shape=jax.ShapeDtypeStruct((2, high, wide), jnp.float32),
        in_specs=[
            smem,
            smem,
            pl.BlockSpec((blocks, 2, share, tile), lambda j: (0, 0, 0, j)),
            whole((high, 1)),
            whole((high, 1)),
            whole((high, 2 * PAN)),
            pl.BlockSpec((tile, 2 * PAN), lambda j: (j, 0)),
            pl.BlockSpec((tile, 2 * PAN), lambda j: (j, 0)),
            whole((high, 2 * SN)),
            smem,
        ],
        out_specs=pl.BlockSpec((2, high, tile), lambda j: (0, 0, j)),
        scratch_shapes=[pltpu.VMEM((high, high), jnp.bfloat16)],
        compiler_params=pltpu.CompilerParams(vmem_limit_bytes=VMEM_LIMIT),
        cost_estimate=pl.CostEstimate(
            flops=8 * high * wide * PAN, bytes_accessed=20_000_000, transcendentals=0
        ),
    )(shift, keep, block, row_places, row_owner, factor, real, imag, own, mine)


def body(hamiltonian, margin, pole_shift, row_map, parent):
    grid_rows = lax.axis_size("prow")
    grid_cols = lax.axis_size("pcol")
    my_row = lax.axis_index("prow")
    my_col = lax.axis_index("pcol")
    share, total = hamiltonian.shape
    wide = total // grid_cols
    high = row_map.shape[0]
    node_count = parent.shape[0]

    both = jnp.stack(
        [
            jnp.stack([m[:, c * wide : (c + 1) * wide] for m in (hamiltonian, margin)])
            for c in range(grid_cols)
        ]
    )
    block = lax.all_to_all(both, "pcol", split_axis=0, concat_axis=0, tiled=True)

    edge = jnp.stack(
        [
            jnp.concatenate([m[:, t * wide : t * wide + SN] for t in range(STEPS)], axis=1)
            for m in (hamiltonian, margin)
        ]
    )
    gathered = line_gather(edge, grid_cols)
    gathered = gathered.transpose(1, 0, 2, 3).reshape(2, high, PAN)
    row_places = row_map - my_row * high
    pick = (row_places[:, None] == jnp.arange(high, dtype=jnp.int32)[None, :]).astype(jnp.bfloat16)
    panel = jnp.einsum("nm,pmk->pnk", pick, gathered, preferred_element_type=jnp.float32).astype(
        jnp.bfloat16
    )
    groups = next(g for g in range(1, grid_rows + 1) if g * grid_cols % grid_rows == 0)
    spread = tree(panel, grid_rows, groups, grid_cols)

    slots = []
    for k in range(wide // SN):
        item = spread[k % groups]
        if grid_rows % grid_cols == 0:
            slot = k * grid_cols // grid_rows
            slots.append(item[:, slot * SN : (slot + 1) * SN])
        else:
            slot = (k * grid_cols + my_col) // grid_rows
            slots.append(lax.dynamic_slice_in_dim(item, slot * SN, SN, axis=1))
    pattern = structure(parent, node_count)
    row_nodes = jnp.arange(high // SN, dtype=jnp.int32) * grid_rows + my_row
    col_nodes = jnp.arange(wide // SN, dtype=jnp.int32) * grid_cols + my_col
    all_nodes = jnp.arange(node_count, dtype=jnp.int32)
    pick_rows = (row_nodes[:, None] == all_nodes[None, :]).astype(jnp.float32)
    pick_cols = (col_nodes[:, None] == all_nodes[None, :]).astype(jnp.float32)
    keep = jnp.dot(jnp.dot(pick_rows, pattern), pick_cols.T)

    def shifted(raw, owners):
        rows = raw.shape[1]
        mask = jnp.dot(
            (owners[:, None] == all_nodes[None, :]).astype(jnp.float32), pattern[:, :STEPS]
        )
        mask = jnp.repeat(mask, SN, axis=0)[:, :, None]
        ham = raw[0].astype(jnp.float32).reshape(rows, STEPS, SN)
        over = raw[1].astype(jnp.float32).reshape(rows, STEPS, SN)
        real = jnp.where(mask > 0.5, ham - pole_shift[0] * over, 0.0)
        imag = jnp.where(mask > 0.5, -pole_shift[1] * over, 0.0)
        return jnp.stack([real, imag], axis=2).reshape(rows, 2 * PAN)

    pivot = shifted(jnp.concatenate(spread[groups:], axis=1), all_nodes[:STEPS])
    owners = jnp.concatenate([row_nodes, col_nodes])
    rows = shifted(jnp.concatenate([panel] + slots, axis=1), owners)
    nodes = jnp.repeat(owners, SN)[:, None]
    factor, real, imag = panels(pivot, nodes, rows, high, wide)
    step = jnp.minimum(my_col, STEPS - 1)
    own = lax.dynamic_slice_in_dim(factor, step * 2 * SN, 2 * SN, axis=1)
    mine = jnp.where(my_col < STEPS, my_col, node_count).astype(jnp.int32).reshape(1)
    return update(
        pole_shift, keep, block, row_places[:, None], nodes[:high], factor, real, imag, own, mine
    )


def solution(mesh):
    return jax.shard_map(
        body,
        mesh=mesh,
        in_specs=(P(("prow", "pcol"), None), P(("prow", "pcol"), None), P("pole"), P("prow"), P()),
        out_specs=P("pole", "prow", "pcol"),
        check_vma=False,
    )
```

```python
import functools

import jax
import jax.numpy as jnp
from jax import lax
from jax.experimental import pallas as pl
from jax.experimental.pallas import tpu as pltpu
from jax.sharding import PartitionSpec as P

SN = 128
STEPS = 3
NSI = 4
PAN = STEPS * SN
PARTS = 4
VMEM_LIMIT = 50 * 1024 * 1024
MESH = pl.DeviceIdType.MESH


def structure(parent, node_count):
    node_index = jnp.arange(node_count, dtype=jnp.int32)
    reached = (parent[:, None] == node_index[None, :]).astype(jnp.bfloat16)
    for level_index in range(node_count.bit_length()):
        hop = jnp.dot(reached, reached, preferred_element_type=jnp.float32)
        reached = jnp.minimum(reached.astype(jnp.float32) + hop, 1.0).astype(jnp.bfloat16)
    reached = reached.astype(jnp.float32)
    same = (node_index[:, None] == node_index[None, :]).astype(jnp.float32)
    return jnp.minimum(same + reached + reached.T, 1.0)


def line_gather_kernel(n, mine_ref, out_ref, local_sem, up_sem, down_sem, recv_sem):
    me = lax.axis_index("pcol")
    row = lax.axis_index("prow")
    pole = lax.axis_index("pole")
    barrier = pltpu.get_barrier_semaphore()

    @pl.when(me + 1 < n)
    def _():
        pl.semaphore_signal(barrier, inc=1, device_id=(pole, row, me + 1), device_id_type=MESH)

    @pl.when(me >= 1)
    def _():
        pl.semaphore_signal(barrier, inc=1, device_id=(pole, row, me - 1), device_id_type=MESH)

    pl.semaphore_wait(barrier, jnp.where(me + 1 < n, 1, 0) + jnp.where(me >= 1, 1, 0))

    local = pltpu.make_async_copy(mine_ref, out_ref.at[me], local_sem)
    local.start()
    local.wait()

    def send(slot, target, sems):
        return pltpu.make_async_remote_copy(
            src_ref=out_ref.at[slot],
            dst_ref=out_ref.at[slot],
            send_sem=sems.at[slot],
            recv_sem=recv_sem.at[slot],
            device_id=(pole, row, target),
            device_id_type=MESH,
        )

    for step in range(n):
        low = me - step
        high = me + step
        if step:

            @pl.when(low >= 0)
            def _():
                send(low, me, up_sem).wait_recv()

        @pl.when((low >= 0) & (me + 1 < n))
        def _():
            send(low, me + 1, up_sem).start()

        if step:

            @pl.when(high < n)
            def _():
                send(high, me, down_sem).wait_recv()

        @pl.when((high < n) & (me >= 1))
        def _():
            send(high, me - 1, down_sem).start()

    for step in range(n):
        low = me - step
        high = me + step

        @pl.when((low >= 0) & (me + 1 < n))
        def _():
            send(low, me + 1, up_sem).wait_send()

        @pl.when((high < n) & (me >= 1))
        def _():
            send(high, me - 1, down_sem).wait_send()


def line_gather(mine, n):
    return pl.pallas_call(
        functools.partial(line_gather_kernel, n),
        out_shape=jax.ShapeDtypeStruct((n,) + mine.shape, mine.dtype),
        in_specs=[pl.BlockSpec(memory_space=pl.ANY)],
        out_specs=pl.BlockSpec(memory_space=pl.ANY),
        scratch_shapes=[
            pltpu.SemaphoreType.DMA,
            pltpu.SemaphoreType.DMA((n,)),
            pltpu.SemaphoreType.DMA((n,)),
            pltpu.SemaphoreType.DMA((n,)),
        ],
        compiler_params=pltpu.CompilerParams(collective_id=0, has_side_effects=True),
        cost_estimate=pl.CostEstimate(flops=0, bytes_accessed=40_000_000, transcendentals=0),
    )(mine)


def tree_kernel(n, groups, pcols, panel_ref, *rest):
    items = groups + STEPS
    outs = rest[:items]
    local_sem, send_sem, recv_sem = rest[items:]
    me = lax.axis_index("prow")
    col = lax.axis_index("pcol")
    pole = lax.axis_index("pole")
    bits = n.bit_length() - 1
    bit = lambda value, b: (value // (1 << b)) % 2
    partner = lambda b: me + (1 << b) * (1 - 2 * bit(me, b))
    barrier = pltpu.get_barrier_semaphore()
    for b in range(bits):
        pl.semaphore_signal(barrier, inc=1, device_id=(pole, partner(b), col), device_id_type=MESH)
    pl.semaphore_wait(barrier, bits)
    roots = [(col + j * pcols) % n for j in range(groups)] + list(range(STEPS))
    forward = list(range(1, bits)) + [0]
    backward = list(range(bits - 1, 0, -1)) + [0]
    orders = [backward if i % 2 else forward for i in range(items)]
    for i in range(items):

        @pl.when(me == roots[i])
        def _():
            source = panel_ref if i < groups else panel_ref.at[:, 0:SN]
            copy = pltpu.make_async_copy(source, outs[i], local_sem.at[i])
            copy.start()
            copy.wait()

    def view(i, part):
        height = outs[i].shape[1] // PARTS * 2
        return outs[i].at[part % 2, pl.ds(part // 2 * height, height)]

    def send(i, part, stage):
        return pltpu.make_async_remote_copy(
            src_ref=view(i, part),
            dst_ref=view(i, part),
            send_sem=send_sem.at[i, part, stage],
            recv_sem=recv_sem.at[i, part],
            device_id=(pole, partner(orders[i][stage]), col),
            device_id_type=MESH,
        )

    def relative(i, stage):
        return (bit(me, orders[i][stage]) + bit(roots[i], orders[i][stage])) % 2

    def later(i, stage):
        total = 0
        for k in range(stage, bits):
            total = total + relative(i, k)
        return total

    def arrive(i, part, stage):
        @pl.when((relative(i, stage) == 1) & (later(i, stage) == 1))
        def _():
            send(i, part, stage).wait_recv()

    sequence = [(i, part) for i in range(groups, items) for part in range(PARTS)]
    sequence += [(i, part) for part in range(PARTS) for i in range(groups)]
    for stage in range(bits):
        for i, part in sequence:
            if stage:
                arrive(i, part, stage - 1)

            @pl.when(later(i, stage) == 0)
            def _():
                send(i, part, stage).start()

    for i, part in sequence:
        arrive(i, part, bits - 1)
    for stage in range(bits):
        for i, part in sequence:

            @pl.when(later(i, stage) == 0)
            def _():
                send(i, part, stage).wait_send()


def tree(panel, n, groups, pcols):
    bits = n.bit_length() - 1
    items = groups + STEPS
    shapes = [jax.ShapeDtypeStruct(panel.shape, panel.dtype)] * groups + [
        jax.ShapeDtypeStruct((2, SN, PAN), panel.dtype)
    ] * STEPS
    return pl.pallas_call(
        functools.partial(tree_kernel, n, groups, pcols),
        out_shape=shapes,
        in_specs=[pl.BlockSpec(memory_space=pl.ANY)],
        out_specs=[pl.BlockSpec(memory_space=pl.ANY)] * items,
        scratch_shapes=[
            pltpu.SemaphoreType.DMA((items,)),
            pltpu.SemaphoreType.DMA((items, PARTS, bits)),
            pltpu.SemaphoreType.DMA((items, PARTS)),
        ],
        compiler_params=pltpu.CompilerParams(collective_id=1, has_side_effects=True),
        cost_estimate=pl.CostEstimate(flops=0, bytes_accessed=60_000_000, transcendentals=0),
    )(panel)


def real_form(pair):
    left, right = pair[:, :SN], pair[:, SN:]
    return jnp.concatenate([pair, jnp.concatenate([-right, left], axis=1)], axis=0)


def panel_kernel(groups, shift_ref, keep_ref, node_ref, slot_ref, panel_ref, *rest):
    items = rest[:groups]
    pivots = rest[groups : groups + STEPS]
    factor_ref, real_ref, imag_ref, inv, step_b, piv = rest[groups + STEPS :]
    exact = functools.partial(
        jnp.dot, precision=lax.Precision.HIGHEST, preferred_element_type=jnp.float32
    )
    high = panel_ref.shape[1]
    wide = real_ref.shape[0]
    zr, zi = shift_ref[0], shift_ref[1]

    def shifted(ref, span, owner):
        blocks = []
        for t in range(STEPS):
            keep = keep_ref[owner, t] > 0.5
            ham = ref[0, span, t * SN : (t + 1) * SN].astype(jnp.float32)
            over = ref[1, span, t * SN : (t + 1) * SN].astype(jnp.float32)
            pair = jnp.concatenate([ham - zr * over, -zi * over], axis=1)
            blocks.append(jnp.where(keep, pair, 0.0))
        return blocks

    for s in range(STEPS):
        for t, pair in enumerate(shifted(pivots[s], slice(0, SN), s)):
            piv[s * SN : (s + 1) * SN, 2 * t * SN : 2 * (t + 1) * SN] = pair
    place_r = lax.broadcasted_iota(jnp.int32, (SN, SN), 0)
    place_c = lax.broadcasted_iota(jnp.int32, (SN, SN), 1)
    eye = (place_r == place_c).astype(jnp.float32)
    zero = jnp.zeros_like(eye)
    two = 2.0 * real_form(jnp.concatenate([eye, zero], axis=1))
    pairs = [(0, 1), (0, 2), (1, 2)]
    for t in range(STEPS):
        here = slice(t * SN, (t + 1) * SN)
        cols = slice(2 * t * SN, 2 * (t + 1) * SN)
        pivot = piv[here, cols]
        full = real_form(pivot)
        diag_r = jnp.sum(eye * pivot[:, :SN], axis=0, keepdims=True)
        diag_i = jnp.sum(eye * pivot[:, SN:], axis=0, keepdims=True)
        modulus = diag_r * diag_r + diag_i * diag_i
        approx = real_form(
            jnp.concatenate([eye * (diag_r / modulus), eye * (-diag_i / modulus)], axis=1)
        )
        for sweep in range(NSI):
            approx = exact(approx, two - exact(full, approx))
        inv[t] = approx.astype(jnp.bfloat16)
        if t + 1 < STEPS:
            below = slice((t + 1) * SN, STEPS * SN)
            factor = exact(piv[below, cols], approx)
            for t2 in range(t + 1, STEPS):
                cols2 = slice(2 * t2 * SN, 2 * (t2 + 1) * SN)
                link = real_form(piv[here, cols2])
                step_b[pairs.index((t, t2))] = link.astype(jnp.bfloat16)
                piv[below, cols2] = piv[below, cols2] - exact(factor, link)

    def work(ref, slot, owner):
        node = node_ref[owner]
        blocks = shifted(ref, pl.ds(pl.multiple_of(slot * SN, SN), SN), owner)
        factors = []
        kept = []
        for t in range(STEPS):
            below = node > t
            now = blocks[t].astype(jnp.bfloat16)
            factor = jnp.dot(now, inv[t], preferred_element_type=jnp.float32)
            factor = jnp.where(below, factor, 0.0).astype(jnp.bfloat16)
            for t2 in range(t + 1, STEPS):
                blocks[t2] = blocks[t2] - jnp.dot(
                    factor, step_b[pairs.index((t, t2))], preferred_element_type=jnp.float32
                )
            factors.append(factor)
            kept.append(jnp.where(below, blocks[t], 0.0))
        return factors, kept

    @pl.loop(0, high // SN)
    def _(k):
        factors, _ = work(panel_ref, k, STEPS + k)
        for t in range(STEPS):
            span = pl.ds(pl.multiple_of(k * SN, SN), SN)
            factor_ref[span, 2 * t * SN : 2 * (t + 1) * SN] = factors[t]

    for j in range(groups):

        @pl.loop(0, wide // SN // groups)
        def _(m):
            k = m * groups + j
            _, kept = work(items[j], slot_ref[k], STEPS + high // SN + k)
            for t in range(STEPS):
                re, im = kept[t][:, :SN], kept[t][:, SN:]
                span = pl.ds(pl.multiple_of(k * SN, SN), SN)
                cols = slice(2 * t * SN, 2 * (t + 1) * SN)
                real_ref[span, cols] = jnp.concatenate([re, -im], axis=1).astype(jnp.bfloat16)
                imag_ref[span, cols] = jnp.concatenate([im, re], axis=1).astype(jnp.bfloat16)


def panels(shift, keep, owners, slots, panel, spread, groups, wide):
    high = panel.shape[1]
    bf = jnp.bfloat16
    smem = pl.BlockSpec(memory_space=pltpu.SMEM)
    vmem = pl.BlockSpec(memory_space=pltpu.VMEM)
    return pl.pallas_call(
        functools.partial(panel_kernel, groups),
        out_shape=[
            jax.ShapeDtypeStruct((high, 2 * PAN), bf),
            jax.ShapeDtypeStruct((wide, 2 * PAN), bf),
            jax.ShapeDtypeStruct((wide, 2 * PAN), bf),
        ],
        in_specs=[smem] * 4 + [vmem] * (1 + groups + STEPS),
        out_specs=[vmem] * 3,
        scratch_shapes=[
            pltpu.VMEM((STEPS, 2 * SN, 2 * SN), bf),
            pltpu.VMEM((3, 2 * SN, 2 * SN), bf),
            pltpu.VMEM((PAN, 2 * PAN), jnp.float32),
        ],
        compiler_params=pltpu.CompilerParams(vmem_limit_bytes=VMEM_LIMIT),
        cost_estimate=pl.CostEstimate(
            flops=20_000_000_000, bytes_accessed=20_000_000, transcendentals=0
        ),
    )(shift, keep, owners, slots, panel, *spread)


def update_kernel(tile, shift_ref, keep_ref, block_ref, map_ref, node_ref, factor_ref, real_ref, imag_ref, own_ref, mine_ref, out_ref, pick):
    j = pl.program_id(0)
    high = map_ref.shape[0]
    blocks, _, share, _ = block_ref.shape

    @pl.when(j == 0)
    def _():
        place = lax.broadcasted_iota(jnp.int32, (high, high), 1)
        pick[...] = (place == map_ref[...]).astype(jnp.bfloat16)

    nt = (((1,), (1,)), ((), ()))
    factor = factor_ref[...]
    ham = jnp.dot(
        pick[...], block_ref[:, 0].reshape(high, tile), preferred_element_type=jnp.float32
    )
    over = jnp.dot(
        pick[...], block_ref[:, 1].reshape(high, tile), preferred_element_type=jnp.float32
    )
    up_r = lax.dot_general(factor, real_ref[...], nt, preferred_element_type=jnp.float32)
    up_i = lax.dot_general(factor, imag_ref[...], nt, preferred_element_type=jnp.float32)
    zr, zi = shift_ref[0], shift_ref[1]
    for a in range(high // SN):
        for b in range(tile // SN):
            ra, cb = slice(a * SN, (a + 1) * SN), slice(b * SN, (b + 1) * SN)
            keep = keep_ref[a, j * (tile // SN) + b] > 0.5
            h, s = ham[ra, cb], over[ra, cb]
            out_ref[0, ra, cb] = jnp.where(keep, h - zr * s, 0.0) - up_r[ra, cb]
            out_ref[1, ra, cb] = jnp.where(keep, -zi * s, 0.0) - up_i[ra, cb]

    @pl.when(j == 0)
    def _():
        take = node_ref[...] > mine_ref[0]
        for p in range(2):
            own = own_ref[:, p * SN : (p + 1) * SN].astype(jnp.float32)
            out_ref[p, :, 0:SN] = jnp.where(take, own, out_ref[p, :, 0:SN])


def update(shift, keep, block, row_places, row_owner, factor, real, imag, own, mine):
    blocks, _, share, wide = block.shape
    high = blocks * share
    tile = 256
    smem = pl.BlockSpec(memory_space=pltpu.SMEM)
    whole = lambda shape: pl.BlockSpec(shape, lambda j: (0,) * len(shape))
    return pl.pallas_call(
        functools.partial(update_kernel, tile),
        grid=(wide // tile,),
        out_shape=jax.ShapeDtypeStruct((2, high, wide), jnp.float32),
        in_specs=[
            smem,
            smem,
            pl.BlockSpec((blocks, 2, share, tile), lambda j: (0, 0, 0, j)),
            whole((high, 1)),
            whole((high, 1)),
            whole((high, 2 * PAN)),
            pl.BlockSpec((tile, 2 * PAN), lambda j: (j, 0)),
            pl.BlockSpec((tile, 2 * PAN), lambda j: (j, 0)),
            whole((high, 2 * SN)),
            smem,
        ],
        out_specs=pl.BlockSpec((2, high, tile), lambda j: (0, 0, j)),
        scratch_shapes=[pltpu.VMEM((high, high), jnp.bfloat16)],
        compiler_params=pltpu.CompilerParams(vmem_limit_bytes=VMEM_LIMIT),
        cost_estimate=pl.CostEstimate(
            flops=8 * high * wide * PAN, bytes_accessed=20_000_000, transcendentals=0
        ),
    )(shift, keep, block, row_places, row_owner, factor, real, imag, own, mine)


def body(hamiltonian, margin, pole_shift, row_map, parent):
    grid_rows = lax.axis_size("prow")
    grid_cols = lax.axis_size("pcol")
    my_row = lax.axis_index("prow")
    my_col = lax.axis_index("pcol")
    share, total = hamiltonian.shape
    wide = total // grid_cols
    high = row_map.shape[0]
    node_count = parent.shape[0]

    both = jnp.stack(
        [
            jnp.stack([m[:, c * wide : (c + 1) * wide] for m in (hamiltonian, margin)])
            for c in range(grid_cols)
        ]
    )
    edge = jnp.stack(
        [
            jnp.concatenate([m[:, t * wide : t * wide + SN] for t in range(STEPS)], axis=1)
            for m in (hamiltonian, margin)
        ]
    )
    gathered = line_gather(edge, grid_cols)
    gathered, both = lax.optimization_barrier((gathered, both))
    block = lax.all_to_all(both, "pcol", split_axis=0, concat_axis=0, tiled=True)
    gathered = gathered.transpose(1, 0, 2, 3).reshape(2, high, PAN)
    row_places = row_map - my_row * high
    pick = (row_places[:, None] == jnp.arange(high, dtype=jnp.int32)[None, :]).astype(jnp.bfloat16)
    panel = jnp.einsum("nm,pmk->pnk", pick, gathered, preferred_element_type=jnp.float32).astype(
        jnp.bfloat16
    )
    groups = next(g for g in range(1, grid_rows + 1) if g * grid_cols % grid_rows == 0)
    spread = tree(panel, grid_rows, groups, grid_cols)

    pattern = structure(parent, node_count)
    row_nodes = jnp.arange(high // SN, dtype=jnp.int32) * grid_rows + my_row
    col_nodes = jnp.arange(wide // SN, dtype=jnp.int32) * grid_cols + my_col
    all_nodes = jnp.arange(node_count, dtype=jnp.int32)
    pick_rows = (row_nodes[:, None] == all_nodes[None, :]).astype(jnp.float32)
    pick_cols = (col_nodes[:, None] == all_nodes[None, :]).astype(jnp.float32)
    keep = jnp.dot(jnp.dot(pick_rows, pattern), pick_cols.T)

    owners = jnp.concatenate([all_nodes[:STEPS], row_nodes, col_nodes])
    slots = col_nodes // grid_rows
    near = jnp.dot((owners[:, None] == all_nodes[None, :]).astype(jnp.float32), pattern[:, :STEPS])
    factor, real, imag = panels(pole_shift, near, owners, slots, panel, spread, groups, wide)
    row_owner = jnp.repeat(row_nodes, SN)[:, None]
    step = jnp.minimum(my_col, STEPS - 1)
    own = lax.dynamic_slice_in_dim(factor, step * 2 * SN, 2 * SN, axis=1)
    mine = jnp.where(my_col < STEPS, my_col, node_count).astype(jnp.int32).reshape(1)
    return update(
        pole_shift, keep, block, row_places[:, None], row_owner, factor, real, imag, own, mine
    )


def solution(mesh):
    return jax.shard_map(
        body,
        mesh=mesh,
        in_specs=(P(("prow", "pcol"), None), P(("prow", "pcol"), None), P("pole"), P("prow"), P()),
        out_specs=P("pole", "prow", "pcol"),
        check_vma=False,
    )
```

```python
import functools

import jax
import jax.numpy as jnp
from jax import lax
from jax.experimental import pallas as pl
from jax.experimental.pallas import tpu as pltpu
from jax.sharding import PartitionSpec as P

SN = 128
STEPS = 3
NSI = 4
PAN = STEPS * SN
PARTS = 4
VMEM_LIMIT = 50 * 1024 * 1024
MESH = pl.DeviceIdType.MESH


def structure(parent, node_count):
    node_index = jnp.arange(node_count, dtype=jnp.int32)
    reached = (parent[:, None] == node_index[None, :]).astype(jnp.bfloat16)
    for level_index in range(node_count.bit_length()):
        hop = jnp.dot(reached, reached, preferred_element_type=jnp.float32)
        reached = jnp.minimum(reached.astype(jnp.float32) + hop, 1.0).astype(jnp.bfloat16)
    reached = reached.astype(jnp.float32)
    same = (node_index[:, None] == node_index[None, :]).astype(jnp.float32)
    return jnp.minimum(same + reached + reached.T, 1.0)


def line_gather_kernel(n, mine_ref, out_ref, local_sem, send_sem, recv_sem):
    me = lax.axis_index("pcol")
    row = lax.axis_index("prow")
    pole = lax.axis_index("pole")
    barrier = pltpu.get_barrier_semaphore()
    for d in range(1, n):
        pl.semaphore_signal(
            barrier, inc=1, device_id=(pole, row, (me + d) % n), device_id_type=MESH
        )
    pl.semaphore_wait(barrier, n - 1)

    def send(slot, target, d):
        return pltpu.make_async_remote_copy(
            src_ref=mine_ref,
            dst_ref=out_ref.at[slot],
            send_sem=send_sem.at[d],
            recv_sem=recv_sem.at[slot],
            device_id=(pole, row, target),
            device_id_type=MESH,
        )

    for d in range(1, n):
        send(me, (me + d) % n, d).start()
    local = pltpu.make_async_copy(mine_ref, out_ref.at[me], local_sem)
    local.start()
    for d in range(1, n):
        send((me + d) % n, (me + d) % n, d).wait_recv()
    for d in range(1, n):
        send(me, (me + d) % n, d).wait_send()
    local.wait()


def line_gather(mine, n):
    return pl.pallas_call(
        functools.partial(line_gather_kernel, n),
        out_shape=jax.ShapeDtypeStruct((n,) + mine.shape, mine.dtype),
        in_specs=[pl.BlockSpec(memory_space=pl.ANY)],
        out_specs=pl.BlockSpec(memory_space=pl.ANY),
        scratch_shapes=[
            pltpu.SemaphoreType.DMA,
            pltpu.SemaphoreType.DMA((n,)),
            pltpu.SemaphoreType.DMA((n,)),
        ],
        compiler_params=pltpu.CompilerParams(collective_id=0, has_side_effects=True),
        cost_estimate=pl.CostEstimate(flops=0, bytes_accessed=40_000_000, transcendentals=0),
    )(mine)


def tree_kernel(n, groups, pcols, panel_ref, *rest):
    items = groups + STEPS
    outs = rest[:items]
    local_sem, send_sem, recv_sem = rest[items:]
    me = lax.axis_index("prow")
    col = lax.axis_index("pcol")
    pole = lax.axis_index("pole")
    bits = n.bit_length() - 1
    bit = lambda value, b: (value // (1 << b)) % 2
    partner = lambda b: me + (1 << b) * (1 - 2 * bit(me, b))
    barrier = pltpu.get_barrier_semaphore()
    for b in range(bits):
        pl.semaphore_signal(barrier, inc=1, device_id=(pole, partner(b), col), device_id_type=MESH)
    pl.semaphore_wait(barrier, bits)
    roots = [(col + j * pcols) % n for j in range(groups)] + list(range(STEPS))
    forward = list(range(1, bits)) + [0]
    backward = list(range(bits - 1, 0, -1)) + [0]
    orders = [backward if i == groups + 1 else forward for i in range(items)]

    def view(ref, i, part):
        height = outs[i].shape[1] // PARTS * 2
        return ref.at[part % 2, pl.ds(part // 2 * height, height)]

    def send(i, part, stage, source):
        return pltpu.make_async_remote_copy(
            src_ref=view(source, i, part),
            dst_ref=view(outs[i], i, part),
            send_sem=send_sem.at[i, part, stage],
            recv_sem=recv_sem.at[i, part],
            device_id=(pole, partner(orders[i][stage]), col),
            device_id_type=MESH,
        )

    def relative(i, stage):
        return (bit(me, orders[i][stage]) + bit(roots[i], orders[i][stage])) % 2

    def later(i, stage):
        total = 0
        for k in range(stage, bits):
            total = total + relative(i, k)
        return total

    def arrive(i, part, stage):
        @pl.when((relative(i, stage) == 1) & (later(i, stage) == 1))
        def _():
            send(i, part, stage, outs[i]).wait_recv()

    sequence = [(i, part) for i in range(groups, items) for part in range(PARTS)]
    sequence += [(i, part) for part in range(PARTS) for i in range(groups)]
    for stage in range(bits):
        for i, part in sequence:
            if stage:
                arrive(i, part, stage - 1)

            @pl.when(me == roots[i])
            def _():
                send(i, part, stage, panel_ref).start()

            if stage:

                @pl.when((later(i, stage) == 0) & (later(i, 0) > 0))
                def _():
                    send(i, part, stage, outs[i]).start()

    def local(i):
        source = panel_ref if i < groups else panel_ref.at[:, pl.ds(0, SN)]
        return pltpu.make_async_copy(source, outs[i], local_sem.at[i])

    for i in range(items):

        @pl.when(me == roots[i])
        def _():
            local(i).start()

    for i, part in sequence:
        arrive(i, part, bits - 1)
    for stage in range(bits):
        for i, part in sequence:

            @pl.when(later(i, stage) == 0)
            def _():
                send(i, part, stage, outs[i]).wait_send()

    for i in range(items):

        @pl.when(me == roots[i])
        def _():
            local(i).wait()


def tree(panel, n, groups, pcols):
    bits = n.bit_length() - 1
    items = groups + STEPS
    shapes = [jax.ShapeDtypeStruct(panel.shape, panel.dtype)] * groups + [
        jax.ShapeDtypeStruct((2, SN, PAN), panel.dtype)
    ] * STEPS
    return pl.pallas_call(
        functools.partial(tree_kernel, n, groups, pcols),
        out_shape=shapes,
        in_specs=[pl.BlockSpec(memory_space=pl.ANY)],
        out_specs=[pl.BlockSpec(memory_space=pl.ANY)] * items,
        scratch_shapes=[
            pltpu.SemaphoreType.DMA((items,)),
            pltpu.SemaphoreType.DMA((items, PARTS, bits)),
            pltpu.SemaphoreType.DMA((items, PARTS)),
        ],
        compiler_params=pltpu.CompilerParams(collective_id=1, has_side_effects=True),
        cost_estimate=pl.CostEstimate(flops=0, bytes_accessed=60_000_000, transcendentals=0),
    )(panel)


def real_form(pair):
    left, right = pair[:, :SN], pair[:, SN:]
    return jnp.concatenate([pair, jnp.concatenate([-right, left], axis=1)], axis=0)


def panel_kernel(groups, shift_ref, keep_ref, node_ref, slot_ref, panel_ref, *rest):
    items = rest[:groups]
    pivots = rest[groups : groups + STEPS]
    factor_ref, real_ref, imag_ref, inv, step_b, piv = rest[groups + STEPS :]
    exact = functools.partial(
        jnp.dot, precision=lax.Precision.HIGHEST, preferred_element_type=jnp.float32
    )

    def fast(left, right):
        return jnp.dot(
            left.astype(jnp.bfloat16),
            right.astype(jnp.bfloat16),
            preferred_element_type=jnp.float32,
        )

    high = panel_ref.shape[1]
    wide = real_ref.shape[0]
    zr, zi = shift_ref[0], shift_ref[1]

    def shifted(ref, span, owner):
        blocks = []
        for t in range(STEPS):
            keep = keep_ref[owner, t] > 0.5
            ham = ref[0, span, t * SN : (t + 1) * SN].astype(jnp.float32)
            over = ref[1, span, t * SN : (t + 1) * SN].astype(jnp.float32)
            pair = jnp.concatenate([ham - zr * over, -zi * over], axis=1)
            blocks.append(jnp.where(keep, pair, 0.0))
        return blocks

    for s in range(STEPS):
        for t, pair in enumerate(shifted(pivots[s], slice(0, SN), s)):
            piv[s * SN : (s + 1) * SN, 2 * t * SN : 2 * (t + 1) * SN] = pair
    place_r = lax.broadcasted_iota(jnp.int32, (SN, SN), 0)
    place_c = lax.broadcasted_iota(jnp.int32, (SN, SN), 1)
    eye = (place_r == place_c).astype(jnp.float32)
    zero = jnp.zeros_like(eye)
    two = 2.0 * real_form(jnp.concatenate([eye, zero], axis=1))
    pairs = [(0, 1), (0, 2), (1, 2)]
    for t in range(STEPS):
        here = slice(t * SN, (t + 1) * SN)
        cols = slice(2 * t * SN, 2 * (t + 1) * SN)
        pivot = piv[here, cols]
        full = real_form(pivot)
        diag_r = jnp.sum(eye * pivot[:, :SN], axis=0, keepdims=True)
        diag_i = jnp.sum(eye * pivot[:, SN:], axis=0, keepdims=True)
        modulus = diag_r * diag_r + diag_i * diag_i
        approx = real_form(
            jnp.concatenate([eye * (diag_r / modulus), eye * (-diag_i / modulus)], axis=1)
        )
        for sweep in range(NSI):
            product = exact if sweep == NSI - 1 else fast
            approx = product(approx, two - product(full, approx))
        inv[t] = approx.astype(jnp.bfloat16)
        if t + 1 < STEPS:
            below = slice((t + 1) * SN, STEPS * SN)
            factor = exact(piv[below, cols], approx)
            for t2 in range(t + 1, STEPS):
                cols2 = slice(2 * t2 * SN, 2 * (t2 + 1) * SN)
                link = real_form(piv[here, cols2])
                step_b[pairs.index((t, t2))] = link.astype(jnp.bfloat16)
                piv[below, cols2] = piv[below, cols2] - exact(factor, link)

    def work(ref, slot, owner):
        node = node_ref[owner]
        blocks = shifted(ref, pl.ds(pl.multiple_of(slot * SN, SN), SN), owner)
        factors = []
        kept = []
        for t in range(STEPS):
            below = node > t
            now = blocks[t].astype(jnp.bfloat16)
            factor = jnp.dot(now, inv[t], preferred_element_type=jnp.float32)
            factor = jnp.where(below, factor, 0.0).astype(jnp.bfloat16)
            for t2 in range(t + 1, STEPS):
                blocks[t2] = blocks[t2] - jnp.dot(
                    factor, step_b[pairs.index((t, t2))], preferred_element_type=jnp.float32
                )
            factors.append(factor)
            kept.append(jnp.where(below, blocks[t], 0.0))
        return factors, kept

    @pl.loop(0, high // SN)
    def _(k):
        factors, _ = work(panel_ref, k, STEPS + k)
        for t in range(STEPS):
            span = pl.ds(pl.multiple_of(k * SN, SN), SN)
            factor_ref[span, 2 * t * SN : 2 * (t + 1) * SN] = factors[t]

    for j in range(groups):

        @pl.loop(0, wide // SN // groups)
        def _(m):
            k = m * groups + j
            _, kept = work(items[j], slot_ref[k], STEPS + high // SN + k)
            for t in range(STEPS):
                re, im = kept[t][:, :SN], kept[t][:, SN:]
                span = pl.ds(pl.multiple_of(k * SN, SN), SN)
                cols = slice(2 * t * SN, 2 * (t + 1) * SN)
                real_ref[span, cols] = jnp.concatenate([re, -im], axis=1).astype(jnp.bfloat16)
                imag_ref[span, cols] = jnp.concatenate([im, re], axis=1).astype(jnp.bfloat16)


def panels(shift, keep, owners, slots, panel, spread, groups, wide):
    high = panel.shape[1]
    bf = jnp.bfloat16
    smem = pl.BlockSpec(memory_space=pltpu.SMEM)
    vmem = pl.BlockSpec(memory_space=pltpu.VMEM)
    return pl.pallas_call(
        functools.partial(panel_kernel, groups),
        out_shape=[
            jax.ShapeDtypeStruct((high, 2 * PAN), bf),
            jax.ShapeDtypeStruct((wide, 2 * PAN), bf),
            jax.ShapeDtypeStruct((wide, 2 * PAN), bf),
        ],
        in_specs=[smem] * 4 + [vmem] * (1 + groups + STEPS),
        out_specs=[vmem] * 3,
        scratch_shapes=[
            pltpu.VMEM((STEPS, 2 * SN, 2 * SN), bf),
            pltpu.VMEM((3, 2 * SN, 2 * SN), bf),
            pltpu.VMEM((PAN, 2 * PAN), jnp.float32),
        ],
        compiler_params=pltpu.CompilerParams(vmem_limit_bytes=VMEM_LIMIT),
        cost_estimate=pl.CostEstimate(
            flops=20_000_000_000, bytes_accessed=20_000_000, transcendentals=0
        ),
    )(shift, keep, owners, slots, panel, *spread)


def update_kernel(tile, shift_ref, keep_ref, block_ref, map_ref, node_ref, factor_ref, real_ref, imag_ref, own_ref, mine_ref, out_ref, pick):
    j = pl.program_id(0)
    high = map_ref.shape[0]
    blocks, _, share, _ = block_ref.shape

    @pl.when(j == 0)
    def _():
        place = lax.broadcasted_iota(jnp.int32, (high, high), 1)
        pick[...] = (place == map_ref[...]).astype(jnp.bfloat16)

    nt = (((1,), (1,)), ((), ()))
    factor = factor_ref[...]
    ham = jnp.dot(
        pick[...], block_ref[:, 0].reshape(high, tile), preferred_element_type=jnp.float32
    )
    over = jnp.dot(
        pick[...], block_ref[:, 1].reshape(high, tile), preferred_element_type=jnp.float32
    )
    up_r = lax.dot_general(factor, real_ref[...], nt, preferred_element_type=jnp.float32)
    up_i = lax.dot_general(factor, imag_ref[...], nt, preferred_element_type=jnp.float32)
    zr, zi = shift_ref[0], shift_ref[1]
    for a in range(high // SN):
        for b in range(tile // SN):
            ra, cb = slice(a * SN, (a + 1) * SN), slice(b * SN, (b + 1) * SN)
            keep = keep_ref[a, j * (tile // SN) + b] > 0.5
            h, s = ham[ra, cb], over[ra, cb]
            out_ref[0, ra, cb] = jnp.where(keep, h - zr * s, 0.0) - up_r[ra, cb]
            out_ref[1, ra, cb] = jnp.where(keep, -zi * s, 0.0) - up_i[ra, cb]

    @pl.when(j == 0)
    def _():
        take = node_ref[...] > mine_ref[0]
        for p in range(2):
            own = own_ref[:, p * SN : (p + 1) * SN].astype(jnp.float32)
            out_ref[p, :, 0:SN] = jnp.where(take, own, out_ref[p, :, 0:SN])


def update(shift, keep, block, row_places, row_owner, factor, real, imag, own, mine):
    blocks, _, share, wide = block.shape
    high = blocks * share
    tile = 256
    smem = pl.BlockSpec(memory_space=pltpu.SMEM)
    whole = lambda shape: pl.BlockSpec(shape, lambda j: (0,) * len(shape))
    return pl.pallas_call(
        functools.partial(update_kernel, tile),
        grid=(wide // tile,),
        out_shape=jax.ShapeDtypeStruct((2, high, wide), jnp.float32),
        in_specs=[
            smem,
            smem,
            pl.BlockSpec((blocks, 2, share, tile), lambda j: (0, 0, 0, j)),
            whole((high, 1)),
            whole((high, 1)),
            whole((high, 2 * PAN)),
            pl.BlockSpec((tile, 2 * PAN), lambda j: (j, 0)),
            pl.BlockSpec((tile, 2 * PAN), lambda j: (j, 0)),
            whole((high, 2 * SN)),
            smem,
        ],
        out_specs=pl.BlockSpec((2, high, tile), lambda j: (0, 0, j)),
        scratch_shapes=[pltpu.VMEM((high, high), jnp.bfloat16)],
        compiler_params=pltpu.CompilerParams(vmem_limit_bytes=VMEM_LIMIT),
        cost_estimate=pl.CostEstimate(
            flops=8 * high * wide * PAN, bytes_accessed=20_000_000, transcendentals=0
        ),
    )(shift, keep, block, row_places, row_owner, factor, real, imag, own, mine)


def body(hamiltonian, margin, pole_shift, row_map, parent):
    grid_rows = lax.axis_size("prow")
    grid_cols = lax.axis_size("pcol")
    my_row = lax.axis_index("prow")
    my_col = lax.axis_index("pcol")
    share, total = hamiltonian.shape
    wide = total // grid_cols
    high = row_map.shape[0]
    node_count = parent.shape[0]

    both = jnp.stack(
        [
            jnp.stack([m[:, c * wide : (c + 1) * wide] for m in (hamiltonian, margin)])
            for c in range(grid_cols)
        ]
    )
    edge = jnp.stack(
        [
            jnp.concatenate([m[:, t * wide : t * wide + SN] for t in range(STEPS)], axis=1)
            for m in (hamiltonian, margin)
        ]
    )
    gathered = line_gather(edge, grid_cols)
    gathered, both = lax.optimization_barrier((gathered, both))
    block = lax.all_to_all(both, "pcol", split_axis=0, concat_axis=0, tiled=True)
    gathered = gathered.transpose(1, 0, 2, 3).reshape(2, high, PAN)
    row_places = row_map - my_row * high
    pick = (row_places[:, None] == jnp.arange(high, dtype=jnp.int32)[None, :]).astype(jnp.bfloat16)
    panel = jnp.einsum("nm,pmk->pnk", pick, gathered, preferred_element_type=jnp.float32).astype(
        jnp.bfloat16
    )
    groups = next(g for g in range(1, grid_rows + 1) if g * grid_cols % grid_rows == 0)
    spread = tree(panel, grid_rows, groups, grid_cols)

    pattern = structure(parent, node_count)
    row_nodes = jnp.arange(high // SN, dtype=jnp.int32) * grid_rows + my_row
    col_nodes = jnp.arange(wide // SN, dtype=jnp.int32) * grid_cols + my_col
    all_nodes = jnp.arange(node_count, dtype=jnp.int32)
    pick_rows = (row_nodes[:, None] == all_nodes[None, :]).astype(jnp.float32)
    pick_cols = (col_nodes[:, None] == all_nodes[None, :]).astype(jnp.float32)
    keep = jnp.dot(jnp.dot(pick_rows, pattern), pick_cols.T)

    owners = jnp.concatenate([all_nodes[:STEPS], row_nodes, col_nodes])
    slots = col_nodes // grid_rows
    near = jnp.dot((owners[:, None] == all_nodes[None, :]).astype(jnp.float32), pattern[:, :STEPS])
    factor, real, imag = panels(pole_shift, near, owners, slots, panel, spread, groups, wide)
    row_owner = jnp.repeat(row_nodes, SN)[:, None]
    step = jnp.minimum(my_col, STEPS - 1)
    own = lax.dynamic_slice_in_dim(factor, step * 2 * SN, 2 * SN, axis=1)
    mine = jnp.where(my_col < STEPS, my_col, node_count).astype(jnp.int32).reshape(1)
    return update(
        pole_shift, keep, block, row_places[:, None], row_owner, factor, real, imag, own, mine
    )


def solution(mesh):
    return jax.shard_map(
        body,
        mesh=mesh,
        in_specs=(P(("prow", "pcol"), None), P(("prow", "pcol"), None), P("pole"), P("prow"), P()),
        out_specs=P("pole", "prow", "pcol"),
        check_vma=False,
    )
```

```python
import functools

import jax
import jax.numpy as jnp
from jax import lax
from jax.experimental import pallas as pl
from jax.experimental.pallas import tpu as pltpu
from jax.sharding import PartitionSpec as P

SN = 128
STEPS = 3
NSI = 4
PAN = STEPS * SN
PARTS = 4
VMEM_LIMIT = 50 * 1024 * 1024
MESH = pl.DeviceIdType.MESH


def structure(parent, node_count):
    node_index = jnp.arange(node_count, dtype=jnp.int32)
    reached = (parent[:, None] == node_index[None, :]).astype(jnp.bfloat16)
    for level_index in range(node_count.bit_length()):
        hop = jnp.dot(reached, reached, preferred_element_type=jnp.float32)
        reached = jnp.minimum(reached.astype(jnp.float32) + hop, 1.0).astype(jnp.bfloat16)
    reached = reached.astype(jnp.float32)
    same = (node_index[:, None] == node_index[None, :]).astype(jnp.float32)
    return jnp.minimum(same + reached + reached.T, 1.0)


def real_form(pair):
    left, right = pair[:, :SN], pair[:, SN:]
    return jnp.concatenate([pair, jnp.concatenate([-right, left], axis=1)], axis=0)


def move_kernel(
    n, pcols, groups, shift_ref, keep_ref, map_ref, ham_ref, over_ref,
    block_ref, factor_ref, real_ref, imag_ref,
    edges, pick, panel, inv, step_b, piv, *rest
):
    items = groups + STEPS
    outs = rest[:items]
    edge_sem, line_send, line_recv, own_sem, block_send, block_recv = rest[items : items + 6]
    local_sem, send_sem, recv_sem = rest[items + 6 :]
    me = lax.axis_index("prow")
    col = lax.axis_index("pcol")
    pole = lax.axis_index("pole")
    wide = block_ref.shape[3]
    high = panel.shape[1]
    sources = (ham_ref, over_ref)
    bits = n.bit_length() - 1
    bit = lambda value, b: (value // (1 << b)) % 2
    partner = lambda b: me + (1 << b) * (1 - 2 * bit(me, b))
    barrier = pltpu.get_barrier_semaphore()

    def edge(a, t):
        return pltpu.make_async_copy(
            sources[a].at[:, pl.ds(t * wide, SN)],
            edges.at[col, a, :, pl.ds(t * SN, SN)],
            edge_sem.at[a, t],
        )

    for a in range(2):
        for t in range(STEPS):
            edge(a, t).start()
    for d in range(1, pcols):
        pl.semaphore_signal(
            barrier, inc=1, device_id=(pole, me, (col + d) % pcols), device_id_type=MESH
        )
    for b in range(bits):
        pl.semaphore_signal(barrier, inc=1, device_id=(pole, partner(b), col), device_id_type=MESH)
    for a in range(2):
        for t in range(STEPS):
            edge(a, t).wait()
    pl.semaphore_wait(barrier, pcols - 1 + bits)

    def line(slot, target, d):
        return pltpu.make_async_remote_copy(
            src_ref=edges.at[slot],
            dst_ref=edges.at[slot],
            send_sem=line_send.at[d],
            recv_sem=line_recv.at[slot],
            device_id=(pole, me, target),
            device_id_type=MESH,
        )

    def block(a, column, slot, target, d):
        return pltpu.make_async_remote_copy(
            src_ref=sources[a].at[:, pl.ds(pl.multiple_of(column * wide, SN), wide)],
            dst_ref=block_ref.at[slot, a],
            send_sem=block_send.at[a, d],
            recv_sem=block_recv.at[a, slot],
            device_id=(pole, me, target),
            device_id_type=MESH,
        )

    def own(a):
        return pltpu.make_async_copy(
            sources[a].at[:, pl.ds(pl.multiple_of(col * wide, SN), wide)],
            block_ref.at[col, a],
            own_sem.at[a],
        )

    for d in range(1, pcols):
        line(col, (col + d) % pcols, d).start()
    place = lax.broadcasted_iota(jnp.int32, (high, high), 1)
    pick[...] = (place == map_ref[...]).astype(jnp.bfloat16)
    for d in range(1, pcols):
        line(col, (col + d) % pcols, d).wait_send()
    for d in range(1, pcols):
        for a in range(2):
            block(a, (col + d) % pcols, col, (col + d) % pcols, d).start()
    for a in range(2):
        own(a).start()
    for d in range(1, pcols):
        line((col + d) % pcols, (col + d) % pcols, d).wait_recv()
    for a in range(2):
        panel[a] = jnp.dot(
            pick[...], edges[:, a].reshape(high, PAN), preferred_element_type=jnp.float32
        ).astype(jnp.bfloat16)

    roots = [(col + j * pcols) % n for j in range(groups)] + list(range(STEPS))
    forward = list(range(1, bits)) + [0]
    backward = list(range(bits - 1, 0, -1)) + [0]
    orders = [backward if i == groups + 1 else forward for i in range(items)]

    def view(ref, i, part):
        height = outs[i].shape[1] // PARTS * 2
        return ref.at[part % 2, pl.ds(part // 2 * height, height)]

    def send(i, part, stage, source):
        return pltpu.make_async_remote_copy(
            src_ref=view(source, i, part),
            dst_ref=view(outs[i], i, part),
            send_sem=send_sem.at[i, part, stage],
            recv_sem=recv_sem.at[i, part],
            device_id=(pole, partner(orders[i][stage]), col),
            device_id_type=MESH,
        )

    def relative(i, stage):
        return (bit(me, orders[i][stage]) + bit(roots[i], orders[i][stage])) % 2

    def later(i, stage):
        total = 0
        for k in range(stage, bits):
            total = total + relative(i, k)
        return total

    def arrive(i, part, stage):
        @pl.when((relative(i, stage) == 1) & (later(i, stage) == 1))
        def _():
            send(i, part, stage, outs[i]).wait_recv()

    sequence = [(i, part) for i in range(groups, items) for part in range(PARTS)]
    sequence += [(i, part) for part in range(PARTS) for i in range(groups)]
    for stage in range(bits):
        for i, part in sequence:
            if stage:
                arrive(i, part, stage - 1)

            @pl.when(me == roots[i])
            def _():
                send(i, part, stage, panel).start()

            if stage:

                @pl.when((later(i, stage) == 0) & (later(i, 0) > 0))
                def _():
                    send(i, part, stage, outs[i]).start()

    def local(i):
        source = panel if i < groups else panel.at[:, pl.ds(0, SN)]
        return pltpu.make_async_copy(source, outs[i], local_sem.at[i])

    for i in range(items):

        @pl.when(me == roots[i])
        def _():
            local(i).start()

    for i, part in sequence:
        arrive(i, part, bits - 1)
    for stage in range(bits):
        for i, part in sequence:

            @pl.when(later(i, stage) == 0)
            def _():
                send(i, part, stage, outs[i]).wait_send()

    for i in range(items):

        @pl.when(me == roots[i])
        def _():
            local(i).wait()

    exact = functools.partial(
        jnp.dot, precision=lax.Precision.HIGHEST, preferred_element_type=jnp.float32
    )

    def fast(left, right):
        return jnp.dot(
            left.astype(jnp.bfloat16),
            right.astype(jnp.bfloat16),
            preferred_element_type=jnp.float32,
        )

    zr, zi = shift_ref[0], shift_ref[1]

    def shifted(ref, span, owner):
        blocks = []
        for t in range(STEPS):
            keep = keep_ref[owner, t] > 0.5
            ham = ref[0, span, t * SN : (t + 1) * SN].astype(jnp.float32)
            over = ref[1, span, t * SN : (t + 1) * SN].astype(jnp.float32)
            pair = jnp.concatenate([ham - zr * over, -zi * over], axis=1)
            blocks.append(jnp.where(keep, pair, 0.0))
        return blocks

    for s in range(STEPS):
        for t, pair in enumerate(shifted(outs[groups + s], slice(0, SN), s)):
            piv[s * SN : (s + 1) * SN, 2 * t * SN : 2 * (t + 1) * SN] = pair
    place_r = lax.broadcasted_iota(jnp.int32, (SN, SN), 0)
    place_c = lax.broadcasted_iota(jnp.int32, (SN, SN), 1)
    eye = (place_r == place_c).astype(jnp.float32)
    zero = jnp.zeros_like(eye)
    two = 2.0 * real_form(jnp.concatenate([eye, zero], axis=1))
    pairs = [(0, 1), (0, 2), (1, 2)]
    for t in range(STEPS):
        here = slice(t * SN, (t + 1) * SN)
        cols = slice(2 * t * SN, 2 * (t + 1) * SN)
        pivot = piv[here, cols]
        full = real_form(pivot)
        diag_r = jnp.sum(eye * pivot[:, :SN], axis=0, keepdims=True)
        diag_i = jnp.sum(eye * pivot[:, SN:], axis=0, keepdims=True)
        modulus = diag_r * diag_r + diag_i * diag_i
        approx = real_form(
            jnp.concatenate([eye * (diag_r / modulus), eye * (-diag_i / modulus)], axis=1)
        )
        for sweep in range(NSI):
            product = exact if sweep == NSI - 1 else fast
            approx = product(approx, two - product(full, approx))
        inv[t] = approx.astype(jnp.bfloat16)
        if t + 1 < STEPS:
            below = slice((t + 1) * SN, STEPS * SN)
            factor = exact(piv[below, cols], approx)
            for t2 in range(t + 1, STEPS):
                cols2 = slice(2 * t2 * SN, 2 * (t2 + 1) * SN)
                link = real_form(piv[here, cols2])
                step_b[pairs.index((t, t2))] = link.astype(jnp.bfloat16)
                piv[below, cols2] = piv[below, cols2] - exact(factor, link)

    def work(ref, slot, owner, node):
        blocks = shifted(ref, pl.ds(pl.multiple_of(slot * SN, SN), SN), owner)
        factors = []
        kept = []
        for t in range(STEPS):
            below = node > t
            now = blocks[t].astype(jnp.bfloat16)
            factor = jnp.dot(now, inv[t], preferred_element_type=jnp.float32)
            factor = jnp.where(below, factor, 0.0).astype(jnp.bfloat16)
            for t2 in range(t + 1, STEPS):
                blocks[t2] = blocks[t2] - jnp.dot(
                    factor, step_b[pairs.index((t, t2))], preferred_element_type=jnp.float32
                )
            factors.append(factor)
            kept.append(jnp.where(below, blocks[t], 0.0))
        return factors, kept

    @pl.loop(0, high // SN)
    def _(k):
        factors, _ = work(panel, k, STEPS + k, k * n + me)
        for t in range(STEPS):
            span = pl.ds(pl.multiple_of(k * SN, SN), SN)
            factor_ref[span, 2 * t * SN : 2 * (t + 1) * SN] = factors[t]

    for j in range(groups):

        @pl.loop(0, wide // SN // groups)
        def _(m):
            k = m * groups + j
            _, kept = work(outs[j], (k * pcols + col) // n, STEPS + high // SN + k, k * pcols + col)
            for t in range(STEPS):
                re, im = kept[t][:, :SN], kept[t][:, SN:]
                span = pl.ds(pl.multiple_of(k * SN, SN), SN)
                cols = slice(2 * t * SN, 2 * (t + 1) * SN)
                real_ref[span, cols] = jnp.concatenate([re, -im], axis=1).astype(jnp.bfloat16)
                imag_ref[span, cols] = jnp.concatenate([im, re], axis=1).astype(jnp.bfloat16)

    for a in range(2):
        for d in range(1, pcols):
            block(a, (col + d) % pcols, (col + d) % pcols, (col + d) % pcols, d).wait_recv()
    for a in range(2):
        for d in range(1, pcols):
            block(a, (col + d) % pcols, col, (col + d) % pcols, d).wait_send()
    for a in range(2):
        own(a).wait()


def move(shift, keep, row_places, hamiltonian, margin, n, pcols, groups):
    high = row_places.shape[0]
    share, total = hamiltonian.shape
    wide = total // pcols
    bits = n.bit_length() - 1
    items = groups + STEPS
    bf = jnp.bfloat16
    smem = pl.BlockSpec(memory_space=pltpu.SMEM)
    vmem = pl.BlockSpec(memory_space=pltpu.VMEM)
    hbm = pl.BlockSpec(memory_space=pl.ANY)
    dma = pltpu.SemaphoreType.DMA
    return pl.pallas_call(
        functools.partial(move_kernel, n, pcols, groups),
        out_shape=[
            jax.ShapeDtypeStruct((pcols, 2, share, wide), bf),
            jax.ShapeDtypeStruct((high, 2 * PAN), bf),
            jax.ShapeDtypeStruct((wide, 2 * PAN), bf),
            jax.ShapeDtypeStruct((wide, 2 * PAN), bf),
        ],
        in_specs=[smem, smem, vmem, hbm, hbm],
        out_specs=[hbm, vmem, vmem, vmem],
        scratch_shapes=[
            pltpu.VMEM((pcols, 2, share, PAN), bf),
            pltpu.VMEM((high, high), bf),
            pltpu.VMEM((2, high, PAN), bf),
            pltpu.VMEM((STEPS, 2 * SN, 2 * SN), bf),
            pltpu.VMEM((3, 2 * SN, 2 * SN), bf),
            pltpu.VMEM((PAN, 2 * PAN), jnp.float32),
        ]
        + [pltpu.VMEM((2, high, PAN), bf)] * groups
        + [pltpu.VMEM((2, SN, PAN), bf)] * STEPS
        + [
            dma((2, STEPS)),
            dma((pcols,)),
            dma((pcols,)),
            dma((2,)),
            dma((2, pcols)),
            dma((2, pcols)),
            dma((items,)),
            dma((items, PARTS, bits)),
            dma((items, PARTS)),
        ],
        compiler_params=pltpu.CompilerParams(
            collective_id=0, has_side_effects=True, vmem_limit_bytes=VMEM_LIMIT
        ),
    )(shift, keep, row_places, hamiltonian, margin)


def update_kernel(tile, shift_ref, keep_ref, block_ref, map_ref, node_ref, factor_ref, real_ref, imag_ref, own_ref, mine_ref, out_ref, pick):
    j = pl.program_id(0)
    high = map_ref.shape[0]
    blocks, _, share, _ = block_ref.shape

    @pl.when(j == 0)
    def _():
        place = lax.broadcasted_iota(jnp.int32, (high, high), 1)
        pick[...] = (place == map_ref[...]).astype(jnp.bfloat16)

    nt = (((1,), (1,)), ((), ()))
    factor = factor_ref[...]
    ham = jnp.dot(
        pick[...], block_ref[:, 0].reshape(high, tile), preferred_element_type=jnp.float32
    )
    over = jnp.dot(
        pick[...], block_ref[:, 1].reshape(high, tile), preferred_element_type=jnp.float32
    )
    up_r = lax.dot_general(factor, real_ref[...], nt, preferred_element_type=jnp.float32)
    up_i = lax.dot_general(factor, imag_ref[...], nt, preferred_element_type=jnp.float32)
    zr, zi = shift_ref[0], shift_ref[1]
    for a in range(high // SN):
        for b in range(tile // SN):
            ra, cb = slice(a * SN, (a + 1) * SN), slice(b * SN, (b + 1) * SN)
            keep = keep_ref[a, j * (tile // SN) + b] > 0.5
            h, s = ham[ra, cb], over[ra, cb]
            out_ref[0, ra, cb] = jnp.where(keep, h - zr * s, 0.0) - up_r[ra, cb]
            out_ref[1, ra, cb] = jnp.where(keep, -zi * s, 0.0) - up_i[ra, cb]

    @pl.when(j == 0)
    def _():
        take = node_ref[...] > mine_ref[0]
        for p in range(2):
            own = own_ref[:, p * SN : (p + 1) * SN].astype(jnp.float32)
            out_ref[p, :, 0:SN] = jnp.where(take, own, out_ref[p, :, 0:SN])


def update(shift, keep, block, row_places, row_owner, factor, real, imag, own, mine):
    blocks, _, share, wide = block.shape
    high = blocks * share
    tile = 256
    smem = pl.BlockSpec(memory_space=pltpu.SMEM)
    whole = lambda shape: pl.BlockSpec(shape, lambda j: (0,) * len(shape))
    return pl.pallas_call(
        functools.partial(update_kernel, tile),
        grid=(wide // tile,),
        out_shape=jax.ShapeDtypeStruct((2, high, wide), jnp.float32),
        in_specs=[
            smem,
            smem,
            pl.BlockSpec((blocks, 2, share, tile), lambda j: (0, 0, 0, j)),
            whole((high, 1)),
            whole((high, 1)),
            whole((high, 2 * PAN)),
            pl.BlockSpec((tile, 2 * PAN), lambda j: (j, 0)),
            pl.BlockSpec((tile, 2 * PAN), lambda j: (j, 0)),
            whole((high, 2 * SN)),
            smem,
        ],
        out_specs=pl.BlockSpec((2, high, tile), lambda j: (0, 0, j)),
        scratch_shapes=[pltpu.VMEM((high, high), jnp.bfloat16)],
        compiler_params=pltpu.CompilerParams(vmem_limit_bytes=VMEM_LIMIT),
        cost_estimate=pl.CostEstimate(
            flops=8 * high * wide * PAN, bytes_accessed=20_000_000, transcendentals=0
        ),
    )(shift, keep, block, row_places, row_owner, factor, real, imag, own, mine)


def body(hamiltonian, margin, pole_shift, row_map, parent):
    grid_rows = lax.axis_size("prow")
    grid_cols = lax.axis_size("pcol")
    my_row = lax.axis_index("prow")
    my_col = lax.axis_index("pcol")
    share, total = hamiltonian.shape
    wide = total // grid_cols
    high = row_map.shape[0]
    node_count = parent.shape[0]

    row_places = row_map - my_row * high
    groups = next(g for g in range(1, grid_rows + 1) if g * grid_cols % grid_rows == 0)
    pattern = structure(parent, node_count)
    row_nodes = jnp.arange(high // SN, dtype=jnp.int32) * grid_rows + my_row
    col_nodes = jnp.arange(wide // SN, dtype=jnp.int32) * grid_cols + my_col
    all_nodes = jnp.arange(node_count, dtype=jnp.int32)
    pick_rows = (row_nodes[:, None] == all_nodes[None, :]).astype(jnp.float32)
    pick_cols = (col_nodes[:, None] == all_nodes[None, :]).astype(jnp.float32)
    keep = jnp.dot(jnp.dot(pick_rows, pattern), pick_cols.T)

    owners = jnp.concatenate([all_nodes[:STEPS], row_nodes, col_nodes])
    near = jnp.dot((owners[:, None] == all_nodes[None, :]).astype(jnp.float32), pattern[:, :STEPS])
    block, factor, real, imag = move(
        pole_shift, near, row_places[:, None], hamiltonian, margin, grid_rows, grid_cols, groups
    )
    row_owner = jnp.repeat(row_nodes, SN)[:, None]
    step = jnp.minimum(my_col, STEPS - 1)
    own = lax.dynamic_slice_in_dim(factor, step * 2 * SN, 2 * SN, axis=1)
    mine = jnp.where(my_col < STEPS, my_col, node_count).astype(jnp.int32).reshape(1)
    return update(
        pole_shift, keep, block, row_places[:, None], row_owner, factor, real, imag, own, mine
    )


def solution(mesh):
    return jax.shard_map(
        body,
        mesh=mesh,
        in_specs=(P(("prow", "pcol"), None), P(("prow", "pcol"), None), P("pole"), P("prow"), P()),
        out_specs=P("pole", "prow", "pcol"),
        check_vma=False,
    )
```

```python
import functools

import jax
import jax.numpy as jnp
from jax import lax
from jax.experimental import pallas as pl
from jax.experimental.pallas import tpu as pltpu
from jax.sharding import PartitionSpec as P

SN = 128
STEPS = 3
NSI = 4
PAN = STEPS * SN
PARTS = 4
VMEM_LIMIT = 50 * 1024 * 1024
MESH = pl.DeviceIdType.MESH


def structure(parent, node_count):
    node_index = jnp.arange(node_count, dtype=jnp.int32)
    reached = (parent[:, None] == node_index[None, :]).astype(jnp.bfloat16)
    for level_index in range(node_count.bit_length()):
        hop = jnp.dot(reached, reached, preferred_element_type=jnp.float32)
        reached = jnp.minimum(reached.astype(jnp.float32) + hop, 1.0).astype(jnp.bfloat16)
    reached = reached.astype(jnp.float32)
    same = (node_index[:, None] == node_index[None, :]).astype(jnp.float32)
    return jnp.minimum(same + reached + reached.T, 1.0)


def real_form(pair):
    left, right = pair[:, :SN], pair[:, SN:]
    return jnp.concatenate([pair, jnp.concatenate([-right, left], axis=1)], axis=0)


def move_kernel(
    n, pcols, groups, shift_ref, keep_ref, map_ref, ham_ref, over_ref,
    block_ref, factor_ref, real_ref, imag_ref,
    edges, pick, panel, inv, step_b, piv, *rest
):
    items = groups + STEPS
    outs = rest[:items]
    edge_sem, line_send, line_recv, own_sem, block_send, block_recv = rest[items : items + 6]
    local_sem, send_sem, recv_sem = rest[items + 6 :]
    me = lax.axis_index("prow")
    col = lax.axis_index("pcol")
    pole = lax.axis_index("pole")
    wide = block_ref.shape[3]
    high = panel.shape[1]
    sources = (ham_ref, over_ref)
    bits = n.bit_length() - 1
    bit = lambda value, b: (value // (1 << b)) % 2
    partner = lambda b: me + (1 << b) * (1 - 2 * bit(me, b))
    barrier = pltpu.get_barrier_semaphore()

    def edge(a, t):
        return pltpu.make_async_copy(
            sources[a].at[:, pl.ds(t * wide, SN)],
            edges.at[col, a, :, pl.ds(t * SN, SN)],
            edge_sem.at[a, t],
        )

    for a in range(2):
        for t in range(STEPS):
            edge(a, t).start()
    for d in range(1, pcols):
        pl.semaphore_signal(
            barrier, inc=1, device_id=(pole, me, (col + d) % pcols), device_id_type=MESH
        )
    for b in range(bits):
        pl.semaphore_signal(barrier, inc=1, device_id=(pole, partner(b), col), device_id_type=MESH)
    for a in range(2):
        for t in range(STEPS):
            edge(a, t).wait()
    pl.semaphore_wait(barrier, pcols - 1 + bits)

    def line(slot, target, d):
        return pltpu.make_async_remote_copy(
            src_ref=edges.at[slot],
            dst_ref=edges.at[slot],
            send_sem=line_send.at[d],
            recv_sem=line_recv.at[slot],
            device_id=(pole, me, target),
            device_id_type=MESH,
        )

    def block(a, column, slot, target, d):
        return pltpu.make_async_remote_copy(
            src_ref=sources[a].at[:, pl.ds(pl.multiple_of(column * wide, SN), wide)],
            dst_ref=block_ref.at[slot, a],
            send_sem=block_send.at[a, d],
            recv_sem=block_recv.at[a, slot],
            device_id=(pole, me, target),
            device_id_type=MESH,
        )

    def far(d):
        down = pcols - d
        down = down - jnp.where(down <= col, 1, 0)
        up = d - 1
        up = up + jnp.where(up >= col, 1, 0)
        return jnp.where(col < pcols // 2, down, up)

    def own(a):
        return pltpu.make_async_copy(
            sources[a].at[:, pl.ds(pl.multiple_of(col * wide, SN), wide)],
            block_ref.at[col, a],
            own_sem.at[a],
        )

    for d in range(1, pcols):
        line(col, (col + d) % pcols, d).start()
    place = lax.broadcasted_iota(jnp.int32, (high, high), 1)
    pick[...] = (place == map_ref[...]).astype(jnp.bfloat16)
    for d in range(1, pcols):
        line(col, (col + d) % pcols, d).wait_send()
    for d in range(1, pcols):
        for a in range(2):
            block(a, far(d), col, far(d), d).start()
    for a in range(2):
        own(a).start()
    for d in range(1, pcols):
        line((col + d) % pcols, (col + d) % pcols, d).wait_recv()
    for a in range(2):
        panel[a] = jnp.dot(
            pick[...], edges[:, a].reshape(high, PAN), preferred_element_type=jnp.float32
        ).astype(jnp.bfloat16)

    roots = [(col + j * pcols) % n for j in range(groups)] + list(range(STEPS))
    forward = list(range(1, bits)) + [0]
    backward = list(range(bits - 1, 0, -1)) + [0]
    orders = [backward if i == groups + 1 else forward for i in range(items)]

    def view(ref, i, part):
        height = outs[i].shape[1] // PARTS * 2
        return ref.at[part % 2, pl.ds(part // 2 * height, height)]

    def send(i, part, stage, source):
        return pltpu.make_async_remote_copy(
            src_ref=view(source, i, part),
            dst_ref=view(outs[i], i, part),
            send_sem=send_sem.at[i, part, stage],
            recv_sem=recv_sem.at[i, part],
            device_id=(pole, partner(orders[i][stage]), col),
            device_id_type=MESH,
        )

    def relative(i, stage):
        return (bit(me, orders[i][stage]) + bit(roots[i], orders[i][stage])) % 2

    def later(i, stage):
        total = 0
        for k in range(stage, bits):
            total = total + relative(i, k)
        return total

    def arrive(i, part, stage):
        @pl.when((relative(i, stage) == 1) & (later(i, stage) == 1))
        def _():
            send(i, part, stage, outs[i]).wait_recv()

    sequence = [(i, part) for i in range(groups, items) for part in range(PARTS)]
    sequence += [(i, part) for part in range(PARTS) for i in range(groups)]
    for stage in range(bits):
        for i, part in sequence:
            if stage:
                arrive(i, part, stage - 1)

            @pl.when(me == roots[i])
            def _():
                send(i, part, stage, panel).start()

            if stage:

                @pl.when((later(i, stage) == 0) & (later(i, 0) > 0))
                def _():
                    send(i, part, stage, outs[i]).start()

    def local(i):
        source = panel if i < groups else panel.at[:, pl.ds(0, SN)]
        return pltpu.make_async_copy(source, outs[i], local_sem.at[i])

    for i in range(items):

        @pl.when(me == roots[i])
        def _():
            local(i).start()

    for i, part in sequence:
        arrive(i, part, bits - 1)
    for stage in range(bits):
        for i, part in sequence:

            @pl.when(later(i, stage) == 0)
            def _():
                send(i, part, stage, outs[i]).wait_send()

    for i in range(items):

        @pl.when(me == roots[i])
        def _():
            local(i).wait()

    exact = functools.partial(
        jnp.dot, precision=lax.Precision.HIGHEST, preferred_element_type=jnp.float32
    )

    def fast(left, right):
        return jnp.dot(
            left.astype(jnp.bfloat16),
            right.astype(jnp.bfloat16),
            preferred_element_type=jnp.float32,
        )

    zr, zi = shift_ref[0], shift_ref[1]

    def shifted(ref, span, owner):
        blocks = []
        for t in range(STEPS):
            keep = keep_ref[owner, t] > 0.5
            ham = ref[0, span, t * SN : (t + 1) * SN].astype(jnp.float32)
            over = ref[1, span, t * SN : (t + 1) * SN].astype(jnp.float32)
            pair = jnp.concatenate([ham - zr * over, -zi * over], axis=1)
            blocks.append(jnp.where(keep, pair, 0.0))
        return blocks

    for s in range(STEPS):
        for t, pair in enumerate(shifted(outs[groups + s], slice(0, SN), s)):
            piv[s * SN : (s + 1) * SN, 2 * t * SN : 2 * (t + 1) * SN] = pair
    place_r = lax.broadcasted_iota(jnp.int32, (SN, SN), 0)
    place_c = lax.broadcasted_iota(jnp.int32, (SN, SN), 1)
    eye = (place_r == place_c).astype(jnp.float32)
    zero = jnp.zeros_like(eye)
    two = 2.0 * real_form(jnp.concatenate([eye, zero], axis=1))
    pairs = [(0, 1), (0, 2), (1, 2)]
    for t in range(STEPS):
        here = slice(t * SN, (t + 1) * SN)
        cols = slice(2 * t * SN, 2 * (t + 1) * SN)
        pivot = piv[here, cols]
        full = real_form(pivot)
        diag_r = jnp.sum(eye * pivot[:, :SN], axis=0, keepdims=True)
        diag_i = jnp.sum(eye * pivot[:, SN:], axis=0, keepdims=True)
        modulus = diag_r * diag_r + diag_i * diag_i
        approx = real_form(
            jnp.concatenate([eye * (diag_r / modulus), eye * (-diag_i / modulus)], axis=1)
        )
        for sweep in range(NSI):
            product = exact if sweep == NSI - 1 else fast
            approx = product(approx, two - product(full, approx))
        inv[t] = approx.astype(jnp.bfloat16)
        if t + 1 < STEPS:
            below = slice((t + 1) * SN, STEPS * SN)
            factor = exact(piv[below, cols], approx)
            for t2 in range(t + 1, STEPS):
                cols2 = slice(2 * t2 * SN, 2 * (t2 + 1) * SN)
                link = real_form(piv[here, cols2])
                step_b[pairs.index((t, t2))] = link.astype(jnp.bfloat16)
                piv[below, cols2] = piv[below, cols2] - exact(factor, link)

    def work(ref, slot, owner, node):
        blocks = shifted(ref, pl.ds(pl.multiple_of(slot * SN, SN), SN), owner)
        factors = []
        kept = []
        for t in range(STEPS):
            below = node > t
            now = blocks[t].astype(jnp.bfloat16)
            factor = jnp.dot(now, inv[t], preferred_element_type=jnp.float32)
            factor = jnp.where(below, factor, 0.0).astype(jnp.bfloat16)
            for t2 in range(t + 1, STEPS):
                blocks[t2] = blocks[t2] - jnp.dot(
                    factor, step_b[pairs.index((t, t2))], preferred_element_type=jnp.float32
                )
            factors.append(factor)
            kept.append(jnp.where(below, blocks[t], 0.0))
        return factors, kept

    @pl.loop(0, high // SN)
    def _(k):
        factors, _ = work(panel, k, STEPS + k, k * n + me)
        for t in range(STEPS):
            span = pl.ds(pl.multiple_of(k * SN, SN), SN)
            factor_ref[span, 2 * t * SN : 2 * (t + 1) * SN] = factors[t]

    for j in range(groups):

        @pl.loop(0, wide // SN // groups)
        def _(m):
            k = m * groups + j
            _, kept = work(outs[j], (k * pcols + col) // n, STEPS + high // SN + k, k * pcols + col)
            for t in range(STEPS):
                re, im = kept[t][:, :SN], kept[t][:, SN:]
                span = pl.ds(pl.multiple_of(k * SN, SN), SN)
                cols = slice(2 * t * SN, 2 * (t + 1) * SN)
                real_ref[span, cols] = jnp.concatenate([re, -im], axis=1).astype(jnp.bfloat16)
                imag_ref[span, cols] = jnp.concatenate([im, re], axis=1).astype(jnp.bfloat16)

    for a in range(2):
        for d in range(1, pcols):
            block(a, (col + d) % pcols, (col + d) % pcols, (col + d) % pcols, d).wait_recv()
    for a in range(2):
        for d in range(1, pcols):
            block(a, far(d), col, far(d), d).wait_send()
    for a in range(2):
        own(a).wait()


def move(shift, keep, row_places, hamiltonian, margin, n, pcols, groups):
    high = row_places.shape[0]
    share, total = hamiltonian.shape
    wide = total // pcols
    bits = n.bit_length() - 1
    items = groups + STEPS
    bf = jnp.bfloat16
    smem = pl.BlockSpec(memory_space=pltpu.SMEM)
    vmem = pl.BlockSpec(memory_space=pltpu.VMEM)
    hbm = pl.BlockSpec(memory_space=pl.ANY)
    dma = pltpu.SemaphoreType.DMA
    return pl.pallas_call(
        functools.partial(move_kernel, n, pcols, groups),
        out_shape=[
            jax.ShapeDtypeStruct((pcols, 2, share, wide), bf),
            jax.ShapeDtypeStruct((high, 2 * PAN), bf),
            jax.ShapeDtypeStruct((wide, 2 * PAN), bf),
            jax.ShapeDtypeStruct((wide, 2 * PAN), bf),
        ],
        in_specs=[smem, smem, vmem, hbm, hbm],
        out_specs=[hbm, vmem, vmem, vmem],
        scratch_shapes=[
            pltpu.VMEM((pcols, 2, share, PAN), bf),
            pltpu.VMEM((high, high), bf),
            pltpu.VMEM((2, high, PAN), bf),
            pltpu.VMEM((STEPS, 2 * SN, 2 * SN), bf),
            pltpu.VMEM((3, 2 * SN, 2 * SN), bf),
            pltpu.VMEM((PAN, 2 * PAN), jnp.float32),
        ]
        + [pltpu.VMEM((2, high, PAN), bf)] * groups
        + [pltpu.VMEM((2, SN, PAN), bf)] * STEPS
        + [
            dma((2, STEPS)),
            dma((pcols,)),
            dma((pcols,)),
            dma((2,)),
            dma((2, pcols)),
            dma((2, pcols)),
            dma((items,)),
            dma((items, PARTS, bits)),
            dma((items, PARTS)),
        ],
        compiler_params=pltpu.CompilerParams(
            collective_id=0, has_side_effects=True, vmem_limit_bytes=VMEM_LIMIT
        ),
    )(shift, keep, row_places, hamiltonian, margin)


def update_kernel(tile, shift_ref, keep_ref, block_ref, map_ref, node_ref, factor_ref, real_ref, imag_ref, own_ref, mine_ref, out_ref, pick):
    j = pl.program_id(0)
    high = map_ref.shape[0]
    blocks, _, share, _ = block_ref.shape

    @pl.when(j == 0)
    def _():
        place = lax.broadcasted_iota(jnp.int32, (high, high), 1)
        pick[...] = (place == map_ref[...]).astype(jnp.bfloat16)

    nt = (((1,), (1,)), ((), ()))
    factor = factor_ref[...]
    ham = jnp.dot(
        pick[...], block_ref[:, 0].reshape(high, tile), preferred_element_type=jnp.float32
    )
    over = jnp.dot(
        pick[...], block_ref[:, 1].reshape(high, tile), preferred_element_type=jnp.float32
    )
    up_r = lax.dot_general(factor, real_ref[...], nt, preferred_element_type=jnp.float32)
    up_i = lax.dot_general(factor, imag_ref[...], nt, preferred_element_type=jnp.float32)
    zr, zi = shift_ref[0], shift_ref[1]
    for a in range(high // SN):
        for b in range(tile // SN):
            ra, cb = slice(a * SN, (a + 1) * SN), slice(b * SN, (b + 1) * SN)
            keep = keep_ref[a, j * (tile // SN) + b] > 0.5
            h, s = ham[ra, cb], over[ra, cb]
            out_ref[0, ra, cb] = jnp.where(keep, h - zr * s, 0.0) - up_r[ra, cb]
            out_ref[1, ra, cb] = jnp.where(keep, -zi * s, 0.0) - up_i[ra, cb]

    @pl.when(j == 0)
    def _():
        take = node_ref[...] > mine_ref[0]
        for p in range(2):
            own = own_ref[:, p * SN : (p + 1) * SN].astype(jnp.float32)
            out_ref[p, :, 0:SN] = jnp.where(take, own, out_ref[p, :, 0:SN])


def update(shift, keep, block, row_places, row_owner, factor, real, imag, own, mine):
    blocks, _, share, wide = block.shape
    high = blocks * share
    tile = 256
    smem = pl.BlockSpec(memory_space=pltpu.SMEM)
    whole = lambda shape: pl.BlockSpec(shape, lambda j: (0,) * len(shape))
    return pl.pallas_call(
        functools.partial(update_kernel, tile),
        grid=(wide // tile,),
        out_shape=jax.ShapeDtypeStruct((2, high, wide), jnp.float32),
        in_specs=[
            smem,
            smem,
            pl.BlockSpec((blocks, 2, share, tile), lambda j: (0, 0, 0, j)),
            whole((high, 1)),
            whole((high, 1)),
            whole((high, 2 * PAN)),
            pl.BlockSpec((tile, 2 * PAN), lambda j: (j, 0)),
            pl.BlockSpec((tile, 2 * PAN), lambda j: (j, 0)),
            whole((high, 2 * SN)),
            smem,
        ],
        out_specs=pl.BlockSpec((2, high, tile), lambda j: (0, 0, j)),
        scratch_shapes=[pltpu.VMEM((high, high), jnp.bfloat16)],
        compiler_params=pltpu.CompilerParams(vmem_limit_bytes=VMEM_LIMIT),
        cost_estimate=pl.CostEstimate(
            flops=8 * high * wide * PAN, bytes_accessed=20_000_000, transcendentals=0
        ),
    )(shift, keep, block, row_places, row_owner, factor, real, imag, own, mine)


def body(hamiltonian, margin, pole_shift, row_map, parent):
    grid_rows = lax.axis_size("prow")
    grid_cols = lax.axis_size("pcol")
    my_row = lax.axis_index("prow")
    my_col = lax.axis_index("pcol")
    share, total = hamiltonian.shape
    wide = total // grid_cols
    high = row_map.shape[0]
    node_count = parent.shape[0]

    row_places = row_map - my_row * high
    groups = next(g for g in range(1, grid_rows + 1) if g * grid_cols % grid_rows == 0)
    pattern = structure(parent, node_count)
    row_nodes = jnp.arange(high // SN, dtype=jnp.int32) * grid_rows + my_row
    col_nodes = jnp.arange(wide // SN, dtype=jnp.int32) * grid_cols + my_col
    all_nodes = jnp.arange(node_count, dtype=jnp.int32)
    pick_rows = (row_nodes[:, None] == all_nodes[None, :]).astype(jnp.float32)
    pick_cols = (col_nodes[:, None] == all_nodes[None, :]).astype(jnp.float32)
    keep = jnp.dot(jnp.dot(pick_rows, pattern), pick_cols.T)

    owners = jnp.concatenate([all_nodes[:STEPS], row_nodes, col_nodes])
    near = jnp.dot((owners[:, None] == all_nodes[None, :]).astype(jnp.float32), pattern[:, :STEPS])
    block, factor, real, imag = move(
        pole_shift, near, row_places[:, None], hamiltonian, margin, grid_rows, grid_cols, groups
    )
    row_owner = jnp.repeat(row_nodes, SN)[:, None]
    step = jnp.minimum(my_col, STEPS - 1)
    own = lax.dynamic_slice_in_dim(factor, step * 2 * SN, 2 * SN, axis=1)
    mine = jnp.where(my_col < STEPS, my_col, node_count).astype(jnp.int32).reshape(1)
    return update(
        pole_shift, keep, block, row_places[:, None], row_owner, factor, real, imag, own, mine
    )


def solution(mesh):
    return jax.shard_map(
        body,
        mesh=mesh,
        in_specs=(P(("prow", "pcol"), None), P(("prow", "pcol"), None), P("pole"), P("prow"), P()),
        out_specs=P("pole", "prow", "pcol"),
        check_vma=False,
    )
```
